256 devices in a mesh: band: 8 (over x, y_lo), grid: 32 (over y_hi, z, core).
Axes of the slice: x: 4, y: 4 (y_hi: 2, y_lo: 2; y = y_hi * 2 + y_lo), z: 8, core: 2. Of those that a mesh axis runs over, the one named last changes fastest.
Arguments:
- orbitals: float32 [16, 128, 128, 128], P('band', 'grid'), may hold values from -3 to 3
Outputs:
- exchange_terms: float32 [16, 128, 128, 128], P('band', 'grid')
The draws below stay inside these ranges and needn't reach their ends.
All inputs are finite; a program needn't handle non-finite values.
Results may differ from the reference program's by a relative error of at most 0.0003.
Values sent between devices are 32-bit elements; how exact they have to be, the bound alone decides.
A program may use at most 64 MiB of HBM per device.

```python
import math
import jax
import jax.numpy as jnp
from jax import lax

NG = 128
ORB = 2
NB = 16
N_BAND = 8


def draw_orbitals(key, part):
    key = jax.random.fold_in(key, 11)
    values = jax.random.truncated_normal(key, -6.0, 6.0, (NB, NG, NG, NG), jnp.float32)
    return (0.5 * values).astype(jnp.float32)


def setup_inputs(seed: int = 0) -> dict:
    splits = jax.random.split(jax.random.key(seed), 2)
    return {
        "orbitals": draw_orbitals(jax.random.fold_in(splits[1], 71), 0),
    }


screening = 0.0428


def signed_freq(index, count):
    return jnp.where(index < count // 2, index, index - count)


def screened_kernel(xindex, yindex, zindex, count):
    scale = 2.0 * math.pi / count
    kx = signed_freq(xindex, count).astype(jnp.float32) * scale
    ky = signed_freq(yindex, count).astype(jnp.float32) * scale
    kz = signed_freq(zindex, count).astype(jnp.float32) * scale
    square = kx * kx + ky * ky + kz * kz
    positive = square > 0
    safe_square = jnp.where(positive, square, 1.0)
    value = -4.0 * math.pi * jnp.expm1(-safe_square / (4.0 * screening * screening)) / safe_square
    return jnp.where(positive, value, math.pi / (screening * screening))


def reference(orbitals):
    points = jnp.arange(NG, dtype=jnp.int32)
    kernel = screened_kernel(points[:, None, None], points[None, :, None], points[None, None, :], NG)
    blocks = orbitals.reshape(N_BAND, ORB, NG, NG, NG)

    def one_group(group):
        own = blocks[group]
        previous = blocks[(group - 1 + N_BAND) % N_BAND]

        def one_column(column):
            partner = previous[column]
            density = own * partner[None]
            spectrum = jnp.fft.fftn(density, axes=(1, 2, 3)) * kernel[None]
            potential = jnp.real(jnp.fft.ifftn(spectrum, axes=(1, 2, 3))).astype(jnp.float32)
            return potential * partner[None], jnp.sum(potential * own, axis=0)

        forward, backward = lax.map(one_column, jnp.arange(ORB, dtype=jnp.int32))
        return jnp.sum(forward, axis=0), backward

    forward, backward = lax.map(one_group, jnp.arange(N_BAND, dtype=jnp.int32))
    returned = jnp.roll(backward, -1, axis=0)
    total = -0.25 * (forward + returned)
    return total.reshape(NB, NG, NG, NG)
```

```python
import functools
import math

import jax
import jax.numpy as jnp
import ml_dtypes
import numpy as np
from jax import lax
from jax.experimental import pallas as pl
from jax.experimental.pallas import tpu as pltpu
from jax.sharding import PartitionSpec as P

screening = 0.0428
MESH = pl.DeviceIdType.MESH
N = 128
LINES = 4
PEERS = 32
BLOCK = 8 * LINES


def complex_matrix(sign):
    points = np.arange(N)
    angle = (points[:, None] * points[None, :] % N) * (2.0 * math.pi / N)
    cosine, sine = np.cos(angle), sign * np.sin(angle)
    return np.block([[cosine, -sine], [sine, cosine]])


def peer_rows():
    peer, part, line = np.meshgrid(np.arange(PEERS), np.arange(2), np.arange(LINES), indexing="ij")
    return (part * N + peer * LINES + line).reshape(-1)


def gathered_rows():
    line, part, peer = np.meshgrid(np.arange(LINES), np.arange(2), np.arange(PEERS), indexing="ij")
    return (part * N + peer * LINES + line).reshape(-1)


def tables():
    forward, inverse = complex_matrix(-1), complex_matrix(1)
    rows, columns = peer_rows(), gathered_rows()
    whole = np.stack(
        [
            forward.T,
            forward[rows],
            forward[:, columns],
            inverse[rows],
            inverse[:, columns],
            inverse.T,
        ]
    ).astype(np.float32)
    high = whole.astype(ml_dtypes.bfloat16)
    low = (whole - high.astype(np.float32)).astype(ml_dtypes.bfloat16)
    return np.stack([high, low], axis=1)


def split(x):
    high = x.astype(jnp.bfloat16)
    return high, (x - high.astype(jnp.float32)).astype(jnp.bfloat16)


def product(a, b):
    dot = functools.partial(jnp.dot, preferred_element_type=jnp.float32)
    return dot(a[0], b[0]) + (dot(a[0], b[1]) + dot(a[1], b[0]))


def signed(index):
    return jnp.where(index < N // 2, index, index - N).astype(jnp.float32) * (2.0 * math.pi / N)


def filter_values(me):
    shape = (N, LINES * N)
    lane = lax.broadcasted_iota(jnp.int32, shape, 1)
    kx = signed(lax.broadcasted_iota(jnp.int32, shape, 0))
    ky = signed(me * LINES + lane // N)
    kz = signed(lane % N)
    square = kx * kx + ky * ky + kz * kz
    positive = square > 0
    safe = jnp.where(positive, square, 1.0)
    value = 4.0 * math.pi * (1.0 - jnp.exp(-safe / (4.0 * screening * screening))) / safe
    value = jnp.where(positive, value, math.pi / (screening * screening))
    return value * (-0.25 / float(N * N * N))


def kernel(
    orb_hbm, table_hbm, out_ref,
    own, table, received, filt, out_a, in_a, out_b, in_b, back, returned,
    local_sem, shift_send, shift_recv, a_send, a_recv, b_send, b_recv, ret_send, ret_recv,
):
    grid, band = lax.axis_index("grid"), lax.axis_index("band")
    following, previous = lax.rem(band + 1, 8), lax.rem(band + 7, 8)
    zone, core, half = grid // 2 % 8, grid % 2, grid // 16

    def peer(k):
        t = k // 4
        step = (t % 2) * ((t + 1) // 2) + (1 - t % 2) * (8 - t // 2)
        return (half + k % 2) % 2 * 16 + (zone + step) % 8 * 2 + (core + k // 2 % 2) % 2

    load_own = pltpu.make_async_copy(orb_hbm, own, local_sem.at[0])
    load_table = pltpu.make_async_copy(table_hbm, table, local_sem.at[1])
    load_own.start()
    load_table.start()

    barrier = pltpu.get_barrier_semaphore()
    pl.semaphore_signal(barrier, inc=1, device_id={"band": following}, device_id_type=MESH)
    pl.semaphore_signal(barrier, inc=1, device_id={"band": previous}, device_id_type=MESH)

    def greet(k, carry):
        pl.semaphore_signal(barrier, inc=1, device_id={"grid": peer(k)}, device_id_type=MESH)
        return carry

    lax.fori_loop(1, PEERS, greet, 0)
    pl.semaphore_wait(barrier, PEERS + 1)

    shifts = []
    for j in range(2):
        copy = pltpu.make_async_remote_copy(
            src_ref=orb_hbm.at[j], dst_ref=received.at[j],
            send_sem=shift_send.at[j], recv_sem=shift_recv.at[j],
            device_id={"band": following}, device_id_type=MESH,
        )
        copy.start()
        shifts.append(copy)

    filt[...] = filter_values(grid)
    load_own.wait()
    load_table.wait()

    def exchange(source, target, send_sem, recv_sem):
        def send(i, carry):
            to = peer(PEERS - 1 - i)
            pltpu.make_async_remote_copy(
                src_ref=source.at[to], dst_ref=target.at[pl.ds(grid * BLOCK, BLOCK)],
                send_sem=send_sem, recv_sem=recv_sem,
                device_id={"grid": to}, device_id_type=MESH,
            ).start()
            return carry

        lax.fori_loop(0, PEERS - 1, send, 0)
        target[pl.ds(pl.multiple_of(grid * BLOCK, BLOCK), BLOCK), :] = source[grid]

    def await_all(target, sem):
        whole = target.at[pl.ds(0, (PEERS - 1) * BLOCK)]
        pltpu.make_async_copy(whole, whole, sem).wait()

    def gathered(target):
        return jnp.concatenate(
            [
                jnp.concatenate(
                    [
                        target[pl.ds(line * 8 + part * LINES + lane, PEERS, stride=BLOCK), :]
                        for line in range(LINES)
                        for part in range(2)
                    ],
                    axis=0,
                )
                for lane in range(LINES)
            ],
            axis=1,
        )

    def weights(index):
        return table[index, 0], table[index, 1]

    def store_blocks(target, value):
        value = value.reshape(PEERS, 8, LINES * N)
        for x in range(LINES):
            target[:, x * 8 : (x + 1) * 8, :] = value[:, :, x * N : (x + 1) * N]

    for j in range(2):
        shifts[j].wait_recv()
        partner = received[j]
        field = jnp.concatenate(
            [(own[c] * partner).reshape(LINES * N, N) for c in range(2)], axis=1
        )
        lines = product(split(field), weights(0))
        planes = jnp.concatenate(
            [
                jnp.concatenate(
                    [lines[x * N : (x + 1) * N, c * N : (c + 1) * N] for x in range(LINES)], axis=1
                )
                for c in range(2)
            ],
            axis=0,
        )
        store_blocks(out_a.at[j], product(weights(1), split(planes)))
        exchange(out_a.at[j], in_a.at[j], a_send.at[j], a_recv.at[j])

    for j in range(2):
        await_all(in_a.at[j], a_recv.at[j])
        spectrum = product(weights(2), split(gathered(in_a.at[j])))
        values = filt[...]
        spectrum = jnp.concatenate([spectrum[:N] * values, spectrum[N:] * values], axis=0)
        store_blocks(out_b.at[j], product(weights(3), split(spectrum)))
        exchange(out_b.at[j], in_b.at[j], b_send.at[j], b_recv.at[j])

    returns = []
    for j in range(2):
        await_all(in_b.at[j], b_recv.at[j])
        planes = product(weights(4), split(gathered(in_b.at[j])))
        lines = jnp.concatenate(
            [
                jnp.concatenate(
                    [planes[c * N : (c + 1) * N, x * N : (x + 1) * N] for c in range(2)], axis=1
                )
                for x in range(LINES)
            ],
            axis=0,
        )
        potential = product(split(lines), weights(5))
        parts = [potential[:, c * N : (c + 1) * N].reshape(LINES, N, N) for c in range(2)]
        back[j] = parts[0] * own[0] + parts[1] * own[1]
        copy = pltpu.make_async_remote_copy(
            src_ref=back.at[j], dst_ref=returned.at[j],
            send_sem=ret_send.at[j], recv_sem=ret_recv.at[j],
            device_id={"band": previous}, device_id_type=MESH,
        )
        copy.start()
        returns.append(copy)
        for c in range(2):
            term = parts[c] * received[j]
            out_ref[c] = term if j == 0 else out_ref[c] + term

    for j in range(2):
        returns[j].wait_recv()
        out_ref[j] += returned[j]

    for j in range(2):
        shifts[j].wait_send()
        returns[j].wait_send()
        await_all(in_a.at[j], a_send.at[j])
        await_all(in_b.at[j], b_send.at[j])


def per_device(orbitals, table):
    slab = (2, LINES, N, N)
    block = (2, PEERS, BLOCK, N)
    flat = (2, PEERS * BLOCK, N)
    f32 = jnp.float32
    return pl.pallas_call(
        kernel,
        out_shape=jax.ShapeDtypeStruct(slab, f32),
        in_specs=[pl.BlockSpec(memory_space=pl.ANY)] * 2,
        out_specs=pl.BlockSpec(memory_space=pltpu.VMEM),
        scratch_shapes=[
            pltpu.VMEM(slab, f32),
            pltpu.VMEM(table.shape, jnp.bfloat16),
            pltpu.VMEM(slab, f32),
            pltpu.VMEM((N, LINES * N), f32),
            pltpu.VMEM(block, f32),
            pltpu.VMEM(flat, f32),
            pltpu.VMEM(block, f32),
            pltpu.VMEM(flat, f32),
            pltpu.VMEM(slab, f32),
            pltpu.VMEM(slab, f32),
        ]
        + [pltpu.SemaphoreType.DMA((2,))] * 9,
        compiler_params=pltpu.CompilerParams(
            collective_id=0, has_side_effects=True, vmem_limit_bytes=48 * 2**20
        ),
    )(orbitals, table)


def solution(mesh):
    body = jax.shard_map(
        per_device,
        mesh=mesh,
        in_specs=(P("band", "grid", None, None), P()),
        out_specs=P("band", "grid", None, None),
        check_vma=False,
    )
    constants = tables()
    return lambda orbitals: body(orbitals, jnp.asarray(constants))
```

```python
import functools
import math

import jax
import jax.numpy as jnp
import numpy as np
from jax import lax
from jax.experimental import pallas as pl
from jax.experimental.pallas import tpu as pltpu
from jax.sharding import PartitionSpec as P

screening = 0.0428
MESH = pl.DeviceIdType.MESH
N = 128
LINES = 4
PEERS = 32
BANDS = 8
BLOCK = 8 * LINES


def complex_matrix(sign):
    points = np.arange(N)
    angle = (points[:, None] * points[None, :] % N) * (2.0 * math.pi / N)
    cosine, sine = np.cos(angle), sign * np.sin(angle)
    return np.block([[cosine, -sine], [sine, cosine]])


def peer_major():
    peer, part, line = np.meshgrid(np.arange(PEERS), np.arange(2), np.arange(LINES), indexing="ij")
    return (part * N + peer * LINES + line).reshape(-1)


def line_major():
    line, part, peer = np.meshgrid(np.arange(LINES), np.arange(2), np.arange(PEERS), indexing="ij")
    return (part * N + peer * LINES + line).reshape(-1)


def tables():
    forward, inverse = complex_matrix(-1), complex_matrix(1)
    peers, lines = peer_major(), line_major()
    return np.stack(
        [
            forward.T,
            forward[peers],
            forward[:, lines],
            inverse[lines],
            inverse[:, lines],
            inverse.T,
        ]
    ).astype(np.float32)


def split(x):
    high = x.astype(jnp.bfloat16)
    return high, (x - high.astype(jnp.float32)).astype(jnp.bfloat16)


def product(a, b):
    dot = functools.partial(jnp.dot, preferred_element_type=jnp.float32)
    return dot(a[0], b[0]) + (dot(a[0], b[1]) + dot(a[1], b[0]))


def signed(index):
    return jnp.where(index < N // 2, index, index - N).astype(jnp.float32) * (2.0 * math.pi / N)


def filter_values(me):
    shape = (N, LINES * N)
    lane = lax.broadcasted_iota(jnp.int32, shape, 1)
    kx = signed(lax.broadcasted_iota(jnp.int32, shape, 0))
    ky = signed(me * LINES + lane // N)
    kz = signed(lane % N)
    square = kx * kx + ky * ky + kz * kz
    positive = square > 0
    safe = jnp.where(positive, square, 1.0)
    value = 4.0 * math.pi * (1.0 - jnp.exp(-safe / (4.0 * screening * screening))) / safe
    value = jnp.where(positive, value, math.pi / (screening * screening))
    return value * (-0.25 / float(N * N * N))


def kernel(
    orb_hbm, table_hbm, forward_hbm, returned_hbm,
    own, exact, table, received, filt, out_a, in_a, out_b, in_b, back, total,
    local_sem, shift_send, shift_recv, a_send, a_recv, b_send, b_recv, ret_send, ret_recv, out_sem,
):
    grid, band = lax.axis_index("grid"), lax.axis_index("band")
    following, previous = lax.rem(band + 1, BANDS), lax.rem(band + BANDS - 1, BANDS)

    load_own = pltpu.make_async_copy(orb_hbm, own, local_sem.at[0])
    load_table = pltpu.make_async_copy(table_hbm, exact, local_sem.at[1])
    load_own.start()
    load_table.start()

    barrier = pltpu.get_barrier_semaphore()
    pl.semaphore_signal(barrier, inc=1, device_id={"band": following}, device_id_type=MESH)
    pl.semaphore_signal(barrier, inc=1, device_id={"band": previous}, device_id_type=MESH)

    def greet(k, carry):
        to = lax.rem(grid + k, PEERS)
        pl.semaphore_signal(barrier, inc=1, device_id={"grid": to}, device_id_type=MESH)
        return carry

    lax.fori_loop(1, PEERS, greet, 0)
    pl.semaphore_wait(barrier, PEERS + 1)

    shifts = []
    for j in range(2):
        for x in range(LINES):
            copy = pltpu.make_async_remote_copy(
                src_ref=orb_hbm.at[j, x], dst_ref=received.at[j, x],
                send_sem=shift_send.at[j, x], recv_sem=shift_recv.at[j, x],
                device_id={"band": following}, device_id_type=MESH,
            )
            copy.start()
            shifts.append(copy)

    filt[...] = filter_values(grid)
    load_own.wait()
    load_table.wait()
    for index in range(6):
        table[index, 0], table[index, 1] = split(exact[index])

    def exchange(source, target, send_sem, recv_sem):
        def send(k, carry):
            to = lax.rem(grid + k, PEERS)
            pltpu.make_async_remote_copy(
                src_ref=source(to), dst_ref=target(grid),
                send_sem=send_sem, recv_sem=recv_sem,
                device_id={"grid": to}, device_id_type=MESH,
            ).start()
            return carry

        lax.fori_loop(1, PEERS, send, 0)

    def await_rows(target, rows, sem):
        some = target.at[pl.ds(0, (PEERS - 1) * rows)]
        pltpu.make_async_copy(some, some, sem).wait()

    def gather(target, units):
        return jnp.concatenate(
            [target[pl.ds(unit, PEERS, stride=BLOCK), :] for unit in units], axis=0
        )

    def weights(index):
        return table[index, 0], table[index, 1]

    def unit(x, part, line):
        return x * 8 + part * LINES + line

    def spectra(j, planes):
        partner = received[j, planes]
        count = partner.shape[0]
        field = jnp.concatenate(
            [(own[c, planes] * partner).reshape(count * N, N) for c in range(2)], axis=1
        )
        lines = product(split(field), weights(0))
        stacked = jnp.concatenate(
            [
                jnp.concatenate(
                    [lines[x * N : (x + 1) * N, c * N : (c + 1) * N] for x in range(count)], axis=1
                )
                for c in range(2)
            ],
            axis=0,
        )
        result = product(weights(1), split(stacked)).reshape(PEERS, 8, count * N)
        for i in range(count):
            x = planes.start + i
            out_a[j, :, x * 8 : (x + 1) * 8, :] = result[:, :, i * N : (i + 1) * N]

    def send_spectra(j, planes):
        rows = pl.ds(planes.start * 8, (planes.stop - planes.start) * 8)
        first = planes.start * 8
        size = (planes.stop - planes.start) * 8
        exchange(
            lambda to: out_a.at[j, to, rows],
            lambda me: in_a.at[j, pl.ds(me * BLOCK + first, size)],
            a_send.at[j], a_recv.at[j],
        )

    def keep(j, target, block):
        target[j, pl.ds(pl.multiple_of(grid * BLOCK, BLOCK), BLOCK), :] = block

    for x in range(LINES):
        shifts[x].wait_recv()
        spectra(0, slice(x, x + 1))
        send_spectra(0, slice(x, x + 1))
    keep(0, in_a, out_a[0, grid])
    for x in range(LINES):
        shifts[LINES + x].wait_recv()
    spectra(1, slice(0, LINES))
    send_spectra(1, slice(0, LINES))
    keep(1, in_a, out_a[1, grid])

    def filtered(j):
        gathered = jnp.concatenate(
            [
                gather(
                    in_a.at[j],
                    [unit(x, part, line) for x in range(LINES) for part in range(2)],
                )
                for line in range(LINES)
            ],
            axis=1,
        )
        spectrum = product(weights(2), split(gathered))
        values = filt[...]
        spectrum = jnp.concatenate([spectrum[:N] * values, spectrum[N:] * values], axis=0)
        result = product(weights(3), split(spectrum))
        target = out_b.at[j]
        for x in range(LINES):
            for part in range(2):
                first = (x * 2 + part) * PEERS
                for line in range(LINES):
                    target[pl.ds(unit(x, part, line), PEERS, stride=BLOCK), :] = result[
                        first : first + PEERS, line * N : (line + 1) * N
                    ]

    def send_filtered(j, x, count, sem):
        size = count * 8
        exchange(
            lambda to: out_b.at[j, pl.ds(to * BLOCK + x * 8, size)],
            lambda me: in_b.at[j, pl.ds(me * BLOCK + x * 8, size)],
            b_send.at[sem], b_recv.at[sem],
        )

    for j in range(2):
        await_rows(in_a.at[j], BLOCK, a_recv.at[j])
        filtered(j)
        if j == 0:
            send_filtered(j, 0, LINES, 0)
        else:
            for x in range(LINES):
                send_filtered(j, x, 1, 1 + x)
        keep(j, in_b, out_b[j, pl.ds(pl.multiple_of(grid * BLOCK, BLOCK), BLOCK), :])

    returns = []
    outputs = []

    def finish(j, x):
        gathered = gather(
            in_b.at[j],
            [unit(x, part, line) for line in range(LINES) for part in range(2)],
        )
        plane = product(weights(4), split(gathered))
        plane = jnp.concatenate([plane[:N], plane[N:]], axis=1)
        potential = product(split(plane), weights(5))
        parts = [potential[:, c * N : (c + 1) * N] for c in range(2)]
        back[j, x] = parts[0] * own[0, x] + parts[1] * own[1, x]
        copy = pltpu.make_async_remote_copy(
            src_ref=back.at[j, x], dst_ref=returned_hbm.at[j, x],
            send_sem=ret_send.at[j, x], recv_sem=ret_recv.at[j, x],
            device_id={"band": previous}, device_id_type=MESH,
        )
        copy.start()
        returns.append(copy)
        for c in range(2):
            term = parts[c] * received[j, x]
            total[c, x] = term if j == 0 else total[c, x] + term
        if j == 1:
            for c in range(2):
                copy = pltpu.make_async_copy(total.at[c, x], forward_hbm.at[c, x], out_sem.at[c, x])
                copy.start()
                outputs.append(copy)

    await_rows(in_b.at[0], BLOCK, b_recv.at[0])
    for x in range(LINES):
        finish(0, x)
    for x in range(LINES):
        await_rows(in_b.at[1], 8, b_recv.at[1 + x])
        finish(1, x)

    for copy in shifts:
        copy.wait_send()
    for j in range(2):
        await_rows(in_a.at[j], BLOCK, a_send.at[j])
    await_rows(in_b.at[0], BLOCK, b_send.at[0])
    for x in range(LINES):
        await_rows(in_b.at[1], 8, b_send.at[1 + x])
    for copy in outputs:
        copy.wait()
    for copy in returns:
        copy.wait()


def per_device(orbitals, table):
    slab = (2, LINES, N, N)
    block = (2, PEERS, BLOCK, N)
    flat = (2, PEERS * BLOCK, N)
    f32 = jnp.float32
    dma = pltpu.SemaphoreType.DMA
    forward, returned = pl.pallas_call(
        kernel,
        out_shape=[jax.ShapeDtypeStruct(slab, f32)] * 2,
        in_specs=[pl.BlockSpec(memory_space=pltpu.HBM)] * 2,
        out_specs=[pl.BlockSpec(memory_space=pltpu.HBM)] * 2,
        scratch_shapes=[
            pltpu.VMEM(slab, f32),
            pltpu.VMEM(table.shape, f32),
            pltpu.VMEM((table.shape[0], 2, 2 * N, 2 * N), jnp.bfloat16),
            pltpu.VMEM(slab, f32),
            pltpu.VMEM((N, LINES * N), f32),
            pltpu.VMEM(block, f32),
            pltpu.VMEM(flat, f32),
            pltpu.VMEM(flat, f32),
            pltpu.VMEM(flat, f32),
            pltpu.VMEM(slab, f32),
            pltpu.VMEM(slab, f32),
            dma((2,)),
            dma((2, LINES)),
            dma((2, LINES)),
            dma((2,)),
            dma((2,)),
            dma((1 + LINES,)),
            dma((1 + LINES,)),
            dma((2, LINES)),
            dma((2, LINES)),
            dma((2, LINES)),
        ],
        compiler_params=pltpu.CompilerParams(
            collective_id=0, has_side_effects=True, vmem_limit_bytes=63 * 2**20
        ),
    )(orbitals, table)
    return forward + returned


def solution(mesh):
    body = jax.shard_map(
        per_device,
        mesh=mesh,
        in_specs=(P("band", "grid", None, None), P()),
        out_specs=P("band", "grid", None, None),
        check_vma=False,
    )
    constants = tables()
    return lambda orbitals: body(orbitals, jnp.asarray(constants))
```

```python
import functools
import math

import jax
import jax.numpy as jnp
import numpy as np
from jax import lax
from jax.experimental import pallas as pl
from jax.experimental.pallas import tpu as pltpu
from jax.sharding import PartitionSpec as P

screening = 0.0428
MESH = pl.DeviceIdType.MESH
N = 128
LINES = 4
PEERS = 32
BANDS = 8
BLOCK = 8 * LINES


def complex_matrix(sign):
    points = np.arange(N)
    angle = (points[:, None] * points[None, :] % N) * (2.0 * math.pi / N)
    cosine, sine = np.cos(angle), sign * np.sin(angle)
    return np.block([[cosine, -sine], [sine, cosine]])


def peer_major():
    peer, part, line = np.meshgrid(np.arange(PEERS), np.arange(2), np.arange(LINES), indexing="ij")
    return (part * N + peer * LINES + line).reshape(-1)


def line_major():
    line, part, peer = np.meshgrid(np.arange(LINES), np.arange(2), np.arange(PEERS), indexing="ij")
    return (part * N + peer * LINES + line).reshape(-1)


def tables():
    forward, inverse = complex_matrix(-1), complex_matrix(1)
    peers, lines = peer_major(), line_major()
    return np.stack(
        [
            forward.T,
            forward[peers],
            forward[:, lines],
            inverse[lines],
            inverse[:, lines],
            inverse.T,
        ]
    ).astype(np.float32)


def split(x):
    high = x.astype(jnp.bfloat16)
    return high, (x - high.astype(jnp.float32)).astype(jnp.bfloat16)


def product(a, b):
    dot = functools.partial(jnp.dot, preferred_element_type=jnp.float32)
    return dot(a[0], b[0]) + (dot(a[0], b[1]) + dot(a[1], b[0]))


def signed(index):
    return jnp.where(index < N // 2, index, index - N).astype(jnp.float32) * (2.0 * math.pi / N)


def filter_values(me):
    shape = (N, LINES * N)
    lane = lax.broadcasted_iota(jnp.int32, shape, 1)
    kx = signed(lax.broadcasted_iota(jnp.int32, shape, 0))
    ky = signed(me * LINES + lane // N)
    kz = signed(lane % N)
    square = kx * kx + ky * ky + kz * kz
    positive = square > 0
    safe = jnp.where(positive, square, 1.0)
    value = 4.0 * math.pi * (1.0 - jnp.exp(-safe / (4.0 * screening * screening))) / safe
    value = jnp.where(positive, value, math.pi / (screening * screening))
    return value * (-0.25 / float(N * N * N))


def kernel(
    orb_hbm, table_hbm, kept_hbm, returned_hbm,
    own, exact, table, received, filt, out_a, in_a, out_b, in_b, back, total,
    table_sem, own_recv, received_recv, shift_send, lent_send,
    a_send, a_recv, b_send, b_recv, ret_send, ret_recv, kept_send, kept_recv,
):
    grid, band = lax.axis_index("grid"), lax.axis_index("band")
    upper, odd = lax.div(grid, PEERS // 2), lax.rem(band, 2)
    partner = band + 1 - 2 * odd
    lower = upper == 0
    upper_even = upper * (1 - odd) == 1
    upper_odd = upper * odd == 1

    def around(by):
        return lax.rem(band + (by + BANDS) % BANDS, BANDS)

    def peer(k):
        to = lax.rem(grid + k, PEERS)
        crosses = lax.rem(lax.div(to, PEERS // 2) + upper, 2)
        return to, {"band": band + crosses * (partner - band), "grid": to}

    load_table = pltpu.make_async_copy(table_hbm, exact, table_sem.at[0])
    load_table.start()

    barrier = pltpu.get_barrier_semaphore()

    def greet_band(to):
        pl.semaphore_signal(barrier, inc=1, device_id={"band": to}, device_id_type=MESH)

    @pl.when(lower)
    def _():
        greet_band(around(1))
        greet_band(around(-1))

    @pl.when(upper == 1)
    def _():
        greet_band(partner)

    @pl.when(upper_odd)
    def _():
        greet_band(around(2))
        greet_band(around(-2))

    def greet(k, carry):
        pl.semaphore_signal(barrier, inc=1, device_id=peer(k)[1], device_id_type=MESH)
        return carry

    lax.fori_loop(1, PEERS, greet, 0)
    pl.semaphore_wait(barrier, PEERS - 1 + (1 - upper) * 2 + upper * (1 + 2 * odd))

    def pass_on(source, target, send_sem, recv_sem, to):
        pltpu.make_async_remote_copy(
            src_ref=source, dst_ref=target, send_sem=send_sem, recv_sem=recv_sem,
            device_id={"band": to}, device_id_type=MESH,
        ).start()

    def stay(source, target, sem):
        pltpu.make_async_copy(source, target, sem).start()

    def await_copy(ref, sem):
        pltpu.make_async_copy(ref, ref, sem).wait()

    pairs = [(c, x) for x in range(LINES) for c in range(2)]
    slabs = [(j, x) for j in range(2) for x in range(LINES)]

    @pl.when(lower)
    def _():
        for j, x in slabs:
            pass_on(
                orb_hbm.at[j, x], received.at[j, x], shift_send.at[0], received_recv.at[j, x], around(1)
            )
        for c, x in pairs:
            stay(orb_hbm.at[c, x], own.at[c, x], own_recv.at[c, x])

    @pl.when(upper == 1)
    def _():
        for c, x in pairs:
            pass_on(orb_hbm.at[c, x], own.at[c, x], shift_send.at[0], own_recv.at[c, x], partner)

    @pl.when(upper_even)
    def _():
        for j, x in slabs:
            stay(orb_hbm.at[j, x], received.at[j, x], received_recv.at[j, x])

    @pl.when(upper_odd)
    def _():
        for j, x in slabs:
            pass_on(
                orb_hbm.at[j, x], received.at[j, x], lent_send.at[0], received_recv.at[j, x], around(2)
            )

    filt[...] = filter_values(grid)
    load_table.wait()
    for index in range(6):
        table[index, 0], table[index, 1] = split(exact[index])

    def exchange(source, target, send_sem, recv_sem):
        def send(k, carry):
            to, device = peer(k)
            pltpu.make_async_remote_copy(
                src_ref=source(to), dst_ref=target(grid),
                send_sem=send_sem, recv_sem=recv_sem,
                device_id=device, device_id_type=MESH,
            ).start()
            return carry

        lax.fori_loop(1, PEERS, send, 0)

    def await_rows(target, rows, sem):
        some = target.at[pl.ds(0, (PEERS - 1) * rows)]
        pltpu.make_async_copy(some, some, sem).wait()

    def gather(target, units):
        return jnp.concatenate(
            [target[pl.ds(unit, PEERS, stride=BLOCK), :] for unit in units], axis=0
        )

    def weights(index):
        return table[index, 0], table[index, 1]

    def unit(x, part, line):
        return x * 8 + part * LINES + line

    def spectra(j, planes):
        partner = received[j, planes]
        count = partner.shape[0]
        field = jnp.concatenate(
            [(own[c, planes] * partner).reshape(count * N, N) for c in range(2)], axis=1
        )
        lines = product(split(field), weights(0))
        stacked = jnp.concatenate(
            [
                jnp.concatenate(
                    [lines[x * N : (x + 1) * N, c * N : (c + 1) * N] for x in range(count)], axis=1
                )
                for c in range(2)
            ],
            axis=0,
        )
        result = product(weights(1), split(stacked)).reshape(PEERS, 8, count * N)
        for i in range(count):
            x = planes.start + i
            out_a[j, :, x * 8 : (x + 1) * 8, :] = result[:, :, i * N : (i + 1) * N]

    def send_spectra(j, planes):
        rows = pl.ds(planes.start * 8, (planes.stop - planes.start) * 8)
        first = planes.start * 8
        size = (planes.stop - planes.start) * 8
        exchange(
            lambda to: out_a.at[j, to, rows],
            lambda me: in_a.at[j, pl.ds(me * BLOCK + first, size)],
            a_send.at[j], a_recv.at[j],
        )

    def keep(j, target, block):
        target[j, pl.ds(pl.multiple_of(grid * BLOCK, BLOCK), BLOCK), :] = block

    for x in range(LINES):
        for c in range(2):
            await_copy(own.at[c, x], own_recv.at[c, x])
        await_copy(received.at[0, x], received_recv.at[0, x])
        spectra(0, slice(x, x + 1))
        send_spectra(0, slice(x, x + 1))
    keep(0, in_a, out_a[0, grid])
    for x in range(LINES):
        await_copy(received.at[1, x], received_recv.at[1, x])
    spectra(1, slice(0, LINES))
    send_spectra(1, slice(0, LINES))
    keep(1, in_a, out_a[1, grid])

    def filtered(j):
        gathered = jnp.concatenate(
            [
                gather(
                    in_a.at[j],
                    [unit(x, part, line) for x in range(LINES) for part in range(2)],
                )
                for line in range(LINES)
            ],
            axis=1,
        )
        spectrum = product(weights(2), split(gathered))
        values = filt[...]
        spectrum = jnp.concatenate([spectrum[:N] * values, spectrum[N:] * values], axis=0)
        result = product(weights(3), split(spectrum))
        target = out_b.at[j]
        for x in range(LINES):
            for part in range(2):
                first = (x * 2 + part) * PEERS
                for line in range(LINES):
                    target[pl.ds(unit(x, part, line), PEERS, stride=BLOCK), :] = result[
                        first : first + PEERS, line * N : (line + 1) * N
                    ]

    def send_filtered(j, x, count, sem):
        size = count * 8
        exchange(
            lambda to: out_b.at[j, pl.ds(to * BLOCK + x * 8, size)],
            lambda me: in_b.at[j, pl.ds(me * BLOCK + x * 8, size)],
            b_send.at[sem], b_recv.at[sem],
        )

    for j in range(2):
        await_rows(in_a.at[j], BLOCK, a_recv.at[j])
        filtered(j)
        if j == 0:
            send_filtered(j, 0, LINES, 0)
        else:
            for x in range(LINES):
                send_filtered(j, x, 1, 1 + x)
        keep(j, in_b, out_b[j, pl.ds(pl.multiple_of(grid * BLOCK, BLOCK), BLOCK), :])

    def finish(j, x):
        gathered = gather(
            in_b.at[j],
            [unit(x, part, line) for line in range(LINES) for part in range(2)],
        )
        plane = product(weights(4), split(gathered))
        plane = jnp.concatenate([plane[:N], plane[N:]], axis=1)
        potential = product(split(plane), weights(5))
        parts = [potential[:, c * N : (c + 1) * N] for c in range(2)]
        back[j, x] = parts[0] * own[0, x] + parts[1] * own[1, x]
        for c in range(2):
            term = parts[c] * received[j, x]
            total[c, x] = term if j == 0 else total[c, x] + term

        @pl.when(lower)
        def _():
            pass_on(back.at[j, x], returned_hbm.at[j, x], ret_send.at[0], ret_recv.at[0], around(-1))
            if j == 1:
                for c in range(2):
                    stay(total.at[c, x], kept_hbm.at[c, x], kept_recv.at[0])

        if j == 1:

            @pl.when(upper == 1)
            def _():
                for c in range(2):
                    pass_on(
                        total.at[c, x], returned_hbm.at[c, x], ret_send.at[0], ret_recv.at[0], partner
                    )

        @pl.when(upper_even)
        def _():
            stay(back.at[j, x], kept_hbm.at[j, x], kept_recv.at[0])

        @pl.when(upper_odd)
        def _():
            pass_on(back.at[j, x], kept_hbm.at[j, x], kept_send.at[0], kept_recv.at[0], around(-2))

    await_rows(in_b.at[0], BLOCK, b_recv.at[0])
    for x in range(LINES):
        finish(0, x)
    for x in range(LINES):
        await_rows(in_b.at[1], 8, b_recv.at[1 + x])
        finish(1, x)

    await_copy(own, shift_send.at[0])
    for j in range(2):
        await_rows(in_a.at[j], BLOCK, a_send.at[j])
    await_rows(in_b.at[0], BLOCK, b_send.at[0])
    for x in range(LINES):
        await_rows(in_b.at[1], 8, b_send.at[1 + x])

    @pl.when(upper_odd)
    def _():
        await_copy(own, lent_send.at[0])
        await_copy(back, kept_send.at[0])

    await_copy(back, ret_send.at[0])
    await_copy(kept_hbm, kept_recv.at[0])
    await_copy(returned_hbm, ret_recv.at[0])


def per_device(orbitals, table):
    slab = (2, LINES, N, N)
    block = (2, PEERS, BLOCK, N)
    flat = (2, PEERS * BLOCK, N)
    f32 = jnp.float32
    dma = pltpu.SemaphoreType.DMA
    kept, returned = pl.pallas_call(
        kernel,
        out_shape=[jax.ShapeDtypeStruct(slab, f32)] * 2,
        in_specs=[pl.BlockSpec(memory_space=pltpu.HBM)] * 2,
        out_specs=[pl.BlockSpec(memory_space=pltpu.HBM)] * 2,
        scratch_shapes=[
            pltpu.VMEM(slab, f32),
            pltpu.VMEM(table.shape, f32),
            pltpu.VMEM((table.shape[0], 2, 2 * N, 2 * N), jnp.bfloat16),
            pltpu.VMEM(slab, f32),
            pltpu.VMEM((N, LINES * N), f32),
            pltpu.VMEM(block, f32),
            pltpu.VMEM(flat, f32),
            pltpu.VMEM(flat, f32),
            pltpu.VMEM(flat, f32),
            pltpu.VMEM(slab, f32),
            pltpu.VMEM(slab, f32),
            dma((1,)),
            dma((2, LINES)),
            dma((2, LINES)),
            dma((1,)),
            dma((1,)),
            dma((2,)),
            dma((2,)),
            dma((1 + LINES,)),
            dma((1 + LINES,)),
            dma((1,)),
            dma((1,)),
            dma((1,)),
            dma((1,)),
        ],
        compiler_params=pltpu.CompilerParams(
            collective_id=0, has_side_effects=True, vmem_limit_bytes=63 * 2**20
        ),
    )(orbitals, table)
    return kept + returned


def solution(mesh):
    body = jax.shard_map(
        per_device,
        mesh=mesh,
        in_specs=(P("band", "grid", None, None), P()),
        out_specs=P("band", "grid", None, None),
        check_vma=False,
    )
    constants = tables()
    return lambda orbitals: body(orbitals, jnp.asarray(constants))
```

```python
import functools
import math

import jax
import jax.numpy as jnp
import numpy as np
from jax import lax
from jax.experimental import pallas as pl
from jax.experimental.pallas import tpu as pltpu
from jax.sharding import PartitionSpec as P

screening = 0.0428
MESH = pl.DeviceIdType.MESH
N = 128
LINES = 4
PEERS = 32
BANDS = 8
BLOCK = 8 * LINES


def complex_matrix(sign):
    points = np.arange(N)
    angle = (points[:, None] * points[None, :] % N) * (2.0 * math.pi / N)
    cosine, sine = np.cos(angle), sign * np.sin(angle)
    return np.block([[cosine, -sine], [sine, cosine]])


def peer_major():
    peer, part, line = np.meshgrid(np.arange(PEERS), np.arange(2), np.arange(LINES), indexing="ij")
    return (part * N + peer * LINES + line).reshape(-1)


def line_major():
    line, part, peer = np.meshgrid(np.arange(LINES), np.arange(2), np.arange(PEERS), indexing="ij")
    return (part * N + peer * LINES + line).reshape(-1)


def tables():
    forward, inverse = complex_matrix(-1), complex_matrix(1)
    peers, lines = peer_major(), line_major()
    return np.stack(
        [
            forward.T,
            forward[peers],
            forward[:, lines],
            inverse[lines],
            inverse[:, lines],
            inverse.T,
        ]
    ).astype(np.float32)


def split(x):
    high = x.astype(jnp.bfloat16)
    return high, (x - high.astype(jnp.float32)).astype(jnp.bfloat16)


def product(a, b):
    dot = functools.partial(jnp.dot, preferred_element_type=jnp.float32)
    return dot(a[0], b[0]) + (dot(a[0], b[1]) + dot(a[1], b[0]))


def signed(index):
    return jnp.where(index < N // 2, index, index - N).astype(jnp.float32) * (2.0 * math.pi / N)


def filter_values(me):
    shape = (N, LINES * N)
    lane = lax.broadcasted_iota(jnp.int32, shape, 1)
    kx = signed(lax.broadcasted_iota(jnp.int32, shape, 0))
    ky = signed(me * LINES + lane // N)
    kz = signed(lane % N)
    square = kx * kx + ky * ky + kz * kz
    positive = square > 0
    safe = jnp.where(positive, square, 1.0)
    value = 4.0 * math.pi * (1.0 - jnp.exp(-safe / (4.0 * screening * screening))) / safe
    value = jnp.where(positive, value, math.pi / (screening * screening))
    return value * (-0.25 / float(N * N * N))


def kernel(
    orb_hbm, table_hbm, kept_hbm, returned_hbm,
    own, exact, table, received, filt, out_a, in_a, out_b, in_b, back, total,
    table_sem, own_recv, received_recv, shift_send, lent_send,
    a_send, a_recv, b_send, b_recv, ret_send, ret_recv, kept_send, kept_recv,
):
    grid, band = lax.axis_index("grid"), lax.axis_index("band")
    upper, odd = lax.div(grid, PEERS // 2), lax.rem(band, 2)
    partner = band + 1 - 2 * odd
    lower = upper == 0
    upper_even = upper * (1 - odd) == 1
    upper_odd = upper * odd == 1

    def around(by):
        return lax.rem(band + (by + BANDS) % BANDS, BANDS)

    half = PEERS // 2
    here, there = upper * half, (1 - upper) * half
    local = grid - here

    def each_peer(visit):
        visit(there + local, partner)

        def step(k, carry):
            place = local + k
            place = jnp.where(place >= half, place - half, place)
            visit(there + place, partner)
            visit(here + place, band)
            return carry

        lax.fori_loop(1, half, step, 0)

    load_table = pltpu.make_async_copy(table_hbm, exact, table_sem.at[0])
    load_table.start()

    barrier = pltpu.get_barrier_semaphore()

    def greet_band(to):
        pl.semaphore_signal(barrier, inc=1, device_id={"band": to}, device_id_type=MESH)

    @pl.when(lower)
    def _():
        greet_band(around(1))
        greet_band(around(-1))

    @pl.when(upper == 1)
    def _():
        greet_band(partner)

    @pl.when(upper_odd)
    def _():
        greet_band(around(2))
        greet_band(around(-2))

    def greet(to, group):
        device = {"band": group, "grid": to}
        pl.semaphore_signal(barrier, inc=1, device_id=device, device_id_type=MESH)

    each_peer(greet)
    pl.semaphore_wait(barrier, PEERS - 1 + (1 - upper) * 2 + upper * (1 + 2 * odd))

    def pass_on(source, target, send_sem, recv_sem, to):
        pltpu.make_async_remote_copy(
            src_ref=source, dst_ref=target, send_sem=send_sem, recv_sem=recv_sem,
            device_id={"band": to}, device_id_type=MESH,
        ).start()

    def stay(source, target, sem):
        pltpu.make_async_copy(source, target, sem).start()

    def await_copy(ref, sem):
        pltpu.make_async_copy(ref, ref, sem).wait()

    pairs = [(c, x) for x in range(LINES) for c in range(2)]
    slabs = [(j, x) for j in range(2) for x in range(LINES)]

    @pl.when(lower)
    def _():
        for j, x in slabs:
            pass_on(
                orb_hbm.at[j, x], received.at[j, x], shift_send.at[0], received_recv.at[j, x], around(1)
            )
        for c, x in pairs:
            stay(orb_hbm.at[c, x], own.at[c, x], own_recv.at[c, x])

    @pl.when(upper == 1)
    def _():
        for c, x in pairs:
            pass_on(orb_hbm.at[c, x], own.at[c, x], shift_send.at[0], own_recv.at[c, x], partner)

    @pl.when(upper_even)
    def _():
        for j, x in slabs:
            stay(orb_hbm.at[j, x], received.at[j, x], received_recv.at[j, x])

    @pl.when(upper_odd)
    def _():
        for j, x in slabs:
            pass_on(
                orb_hbm.at[j, x], received.at[j, x], lent_send.at[0], received_recv.at[j, x], around(2)
            )

    filt[...] = filter_values(grid)
    load_table.wait()
    for index in range(6):
        table[index, 0], table[index, 1] = split(exact[index])

    def exchange(source, target, send_sem, recv_sem):
        def send(to, group):
            pltpu.make_async_remote_copy(
                src_ref=source(to), dst_ref=target(grid),
                send_sem=send_sem, recv_sem=recv_sem,
                device_id={"band": group, "grid": to}, device_id_type=MESH,
            ).start()

        each_peer(send)

    def await_rows(target, rows, sem):
        some = target.at[pl.ds(0, (PEERS - 1) * rows)]
        pltpu.make_async_copy(some, some, sem).wait()

    def gather(target, units):
        return jnp.concatenate(
            [target[pl.ds(unit, PEERS, stride=BLOCK), :] for unit in units], axis=0
        )

    def weights(index):
        return table[index, 0], table[index, 1]

    def unit(x, part, line):
        return x * 8 + part * LINES + line

    def rows_of(x):
        return pl.ds(pl.multiple_of(x * 8, 8), 8)

    def spectra(j, x):
        partner_plane = received[j, x]
        field = jnp.concatenate([own[c, x] * partner_plane for c in range(2)], axis=1)
        lines = product(split(field), weights(0))
        stacked = jnp.concatenate([lines[:, :N], lines[:, N:]], axis=0)
        result = product(weights(1), split(stacked))
        out_a[j, :, rows_of(x), :] = result.reshape(PEERS, 8, N)

    def send_spectra(j, x):
        exchange(
            lambda to: out_a.at[j, to, rows_of(x)],
            lambda me: in_a.at[j, pl.ds(pl.multiple_of(me * BLOCK + x * 8, 8), 8)],
            a_send.at[j], a_recv.at[j],
        )

    def keep(j, target, block):
        target[j, pl.ds(pl.multiple_of(grid * BLOCK, BLOCK), BLOCK), :] = block

    for j in range(2):

        def form(x, carry):
            if j == 0:
                for c in range(2):
                    await_copy(own.at[c, x], own_recv.at[c, x])
            await_copy(received.at[j, x], received_recv.at[j, x])
            spectra(j, x)
            send_spectra(j, x)
            return carry

        lax.fori_loop(0, LINES, form, 0)
        keep(j, in_a, out_a[j, grid])

    def filtered(j):
        gathered = jnp.concatenate(
            [
                gather(
                    in_a.at[j],
                    [unit(x, part, line) for x in range(LINES) for part in range(2)],
                )
                for line in range(LINES)
            ],
            axis=1,
        )
        spectrum = product(weights(2), split(gathered))
        values = filt[...]
        spectrum = jnp.concatenate([spectrum[:N] * values, spectrum[N:] * values], axis=0)
        result = product(weights(3), split(spectrum))
        target = out_b.at[j]
        for x in range(LINES):
            for part in range(2):
                first = (x * 2 + part) * PEERS
                for line in range(LINES):
                    target[pl.ds(unit(x, part, line), PEERS, stride=BLOCK), :] = result[
                        first : first + PEERS, line * N : (line + 1) * N
                    ]

    def send_filtered(j, x, count, sem):
        size = count * 8
        exchange(
            lambda to: out_b.at[j, pl.ds(pl.multiple_of(to * BLOCK + x * 8, 8), size)],
            lambda me: in_b.at[j, pl.ds(pl.multiple_of(me * BLOCK + x * 8, 8), size)],
            b_send.at[sem], b_recv.at[sem],
        )

    for j in range(2):
        await_rows(in_a.at[j], BLOCK, a_recv.at[j])
        filtered(j)
        if j == 0:
            send_filtered(j, 0, LINES, 0)
        else:

            def send_plane(x, carry):
                send_filtered(j, x, 1, 1 + x)
                return carry

            lax.fori_loop(0, LINES, send_plane, 0)
        keep(j, in_b, out_b[j, pl.ds(pl.multiple_of(grid * BLOCK, BLOCK), BLOCK), :])

    def finish(j, x):
        gathered = gather(
            in_b.at[j],
            [unit(x, part, line) for line in range(LINES) for part in range(2)],
        )
        plane = product(weights(4), split(gathered))
        plane = jnp.concatenate([plane[:N], plane[N:]], axis=1)
        potential = product(split(plane), weights(5))
        parts = [potential[:, c * N : (c + 1) * N] for c in range(2)]
        back[j, x] = parts[0] * own[0, x] + parts[1] * own[1, x]
        for c in range(2):
            term = parts[c] * received[j, x]
            total[c, x] = term if j == 0 else total[c, x] + term

        @pl.when(lower)
        def _():
            pass_on(back.at[j, x], returned_hbm.at[j, x], ret_send.at[0], ret_recv.at[0], around(-1))
            if j == 1:
                for c in range(2):
                    stay(total.at[c, x], kept_hbm.at[c, x], kept_recv.at[0])

        if j == 1:

            @pl.when(upper == 1)
            def _():
                for c in range(2):
                    pass_on(
                        total.at[c, x], returned_hbm.at[c, x], ret_send.at[0], ret_recv.at[0], partner
                    )

        @pl.when(upper_even)
        def _():
            stay(back.at[j, x], kept_hbm.at[j, x], kept_recv.at[0])

        @pl.when(upper_odd)
        def _():
            pass_on(back.at[j, x], kept_hbm.at[j, x], kept_send.at[0], kept_recv.at[0], around(-2))

    await_rows(in_b.at[0], BLOCK, b_recv.at[0])
    for j in range(2):

        def close(x, carry):
            if j == 1:
                await_rows(in_b.at[1], 8, b_recv.at[1 + x])
            finish(j, x)
            return carry

        lax.fori_loop(0, LINES, close, 0)

    await_copy(own, shift_send.at[0])
    for j in range(2):
        await_rows(in_a.at[j], BLOCK, a_send.at[j])
    await_rows(in_b.at[0], BLOCK, b_send.at[0])
    for x in range(LINES):
        await_rows(in_b.at[1], 8, b_send.at[1 + x])

    @pl.when(upper_odd)
    def _():
        await_copy(own, lent_send.at[0])
        await_copy(back, kept_send.at[0])

    await_copy(back, ret_send.at[0])
    await_copy(kept_hbm, kept_recv.at[0])
    await_copy(returned_hbm, ret_recv.at[0])


def per_device(orbitals, table):
    slab = (2, LINES, N, N)
    block = (2, PEERS, BLOCK, N)
    flat = (2, PEERS * BLOCK, N)
    f32 = jnp.float32
    dma = pltpu.SemaphoreType.DMA
    kept, returned = pl.pallas_call(
        kernel,
        out_shape=[jax.ShapeDtypeStruct(slab, f32)] * 2,
        in_specs=[pl.BlockSpec(memory_space=pltpu.HBM)] * 2,
        out_specs=[pl.BlockSpec(memory_space=pltpu.HBM)] * 2,
        scratch_shapes=[
            pltpu.VMEM(slab, f32),
            pltpu.VMEM(table.shape, f32),
            pltpu.VMEM((table.shape[0], 2, 2 * N, 2 * N), jnp.bfloat16),
            pltpu.VMEM(slab, f32),
            pltpu.VMEM((N, LINES * N), f32),
            pltpu.VMEM(block, f32),
            pltpu.VMEM(flat, f32),
            pltpu.VMEM(flat, f32),
            pltpu.VMEM(flat, f32),
            pltpu.VMEM(slab, f32),
            pltpu.VMEM(slab, f32),
            dma((1,)),
            dma((2, LINES)),
            dma((2, LINES)),
            dma((1,)),
            dma((1,)),
            dma((2,)),
            dma((2,)),
            dma((1 + LINES,)),
            dma((1 + LINES,)),
            dma((1,)),
            dma((1,)),
            dma((1,)),
            dma((1,)),
        ],
        compiler_params=pltpu.CompilerParams(
            collective_id=0, has_side_effects=True, vmem_limit_bytes=int(52.65 * 2**20)
        ),
    )(orbitals, table)
    return kept + returned


def solution(mesh):
    body = jax.shard_map(
        per_device,
        mesh=mesh,
        in_specs=(P("band", "grid", None, None), P()),
        out_specs=P("band", "grid", None, None),
        check_vma=False,
    )
    constants = tables()
    return lambda orbitals: body(orbitals, jnp.asarray(constants))
```

```python
import functools
import math

import jax
import jax.numpy as jnp
import numpy as np
from jax import lax
from jax.experimental import pallas as pl
from jax.experimental.pallas import tpu as pltpu
from jax.sharding import PartitionSpec as P

screening = 0.0428
MESH = pl.DeviceIdType.MESH
N = 128
LINES = 4
PEERS = 32
BANDS = 8
BLOCK = 8 * LINES


def complex_matrix(sign):
    points = np.arange(N)
    angle = (points[:, None] * points[None, :] % N) * (2.0 * math.pi / N)
    cosine, sine = np.cos(angle), sign * np.sin(angle)
    return np.block([[cosine, -sine], [sine, cosine]])


def peer_major():
    peer, part, line = np.meshgrid(np.arange(PEERS), np.arange(2), np.arange(LINES), indexing="ij")
    return (part * N + peer * LINES + line).reshape(-1)


def line_major():
    line, part, peer = np.meshgrid(np.arange(LINES), np.arange(2), np.arange(PEERS), indexing="ij")
    return (part * N + peer * LINES + line).reshape(-1)


def tables():
    forward, inverse = complex_matrix(-1), complex_matrix(1)
    peers, lines = peer_major(), line_major()
    return np.stack(
        [
            forward.T,
            forward[peers],
            forward[:, lines],
            inverse[lines],
            inverse[:, lines],
            inverse.T,
        ]
    ).astype(np.float32)


def split(x):
    high = x.astype(jnp.bfloat16)
    return high, (x - high.astype(jnp.float32)).astype(jnp.bfloat16)


def product(a, b):
    dot = functools.partial(jnp.dot, preferred_element_type=jnp.float32)
    return dot(a[0], b[0]) + (dot(a[0], b[1]) + dot(a[1], b[0]))


def signed(index):
    return jnp.where(index < N // 2, index, index - N).astype(jnp.float32) * (2.0 * math.pi / N)


def filter_values(me):
    shape = (N, LINES * N)
    lane = lax.broadcasted_iota(jnp.int32, shape, 1)
    kx = signed(lax.broadcasted_iota(jnp.int32, shape, 0))
    ky = signed(me * LINES + lane // N)
    kz = signed(lane % N)
    square = kx * kx + ky * ky + kz * kz
    positive = square > 0
    safe = jnp.where(positive, square, 1.0)
    value = 4.0 * math.pi * (1.0 - jnp.exp(-safe / (4.0 * screening * screening))) / safe
    value = jnp.where(positive, value, math.pi / (screening * screening))
    return value * (-0.25 / float(N * N * N))


def kernel(
    orb_hbm, table_hbm, kept_hbm, returned_hbm,
    own, exact, table, received, filt, out_a, in_a, out_b, in_b, back, total,
    table_sem, own_recv, received_recv, shift_send, lent_send,
    a_send, a_recv, b_send, b_recv, ret_send, ret_recv, kept_send, kept_recv,
):
    grid, band = lax.axis_index("grid"), lax.axis_index("band")
    upper, odd = lax.div(grid, PEERS // 2), lax.rem(band, 2)
    partner = band + 1 - 2 * odd
    lower = upper == 0
    upper_even = upper * (1 - odd) == 1
    upper_odd = upper * odd == 1

    def around(by):
        return lax.rem(band + (by + BANDS) % BANDS, BANDS)

    def peer(k):
        to = lax.rem(grid + k, PEERS)
        crosses = lax.rem(lax.div(to, PEERS // 2) + upper, 2)
        return to, {"band": band + crosses * (partner - band), "grid": to}

    load_table = pltpu.make_async_copy(table_hbm, exact, table_sem.at[0])
    load_table.start()

    barrier = pltpu.get_barrier_semaphore()

    def greet_band(to):
        pl.semaphore_signal(barrier, inc=1, device_id={"band": to}, device_id_type=MESH)

    @pl.when(lower)
    def _():
        greet_band(around(1))
        greet_band(around(-1))

    @pl.when(upper == 1)
    def _():
        greet_band(partner)

    @pl.when(upper_odd)
    def _():
        greet_band(around(2))
        greet_band(around(-2))

    def greet(k, carry):
        pl.semaphore_signal(barrier, inc=1, device_id=peer(k)[1], device_id_type=MESH)
        return carry

    lax.fori_loop(1, PEERS, greet, 0)
    pl.semaphore_wait(barrier, PEERS - 1 + (1 - upper) * 2 + upper * (1 + 2 * odd))

    def pass_on(source, target, send_sem, recv_sem, to):
        pltpu.make_async_remote_copy(
            src_ref=source, dst_ref=target, send_sem=send_sem, recv_sem=recv_sem,
            device_id={"band": to}, device_id_type=MESH,
        ).start()

    def stay(source, target, sem):
        pltpu.make_async_copy(source, target, sem).start()

    def await_copy(ref, sem):
        pltpu.make_async_copy(ref, ref, sem).wait()

    pairs = [(c, x) for x in range(LINES) for c in range(2)]
    slabs = [(j, x) for j in range(2) for x in range(LINES)]

    @pl.when(lower)
    def _():
        for j, x in slabs:
            pass_on(
                orb_hbm.at[j, x], received.at[j, x], shift_send.at[0], received_recv.at[j, x], around(1)
            )
        for c, x in pairs:
            stay(orb_hbm.at[c, x], own.at[c, x], own_recv.at[c, x])

    @pl.when(upper == 1)
    def _():
        for c, x in pairs:
            pass_on(orb_hbm.at[c, x], own.at[c, x], shift_send.at[0], own_recv.at[c, x], partner)

    @pl.when(upper_even)
    def _():
        for j, x in slabs:
            stay(orb_hbm.at[j, x], received.at[j, x], received_recv.at[j, x])

    @pl.when(upper_odd)
    def _():
        for j, x in slabs:
            pass_on(
                orb_hbm.at[j, x], received.at[j, x], lent_send.at[0], received_recv.at[j, x], around(2)
            )

    filt[...] = filter_values(grid)
    load_table.wait()
    for index in range(6):
        table[index, 0], table[index, 1] = split(exact[index])

    def exchange(source, target, send_sem, recv_sem):
        def send(k, carry):
            to, device = peer(k)
            pltpu.make_async_remote_copy(
                src_ref=source(to), dst_ref=target(grid),
                send_sem=send_sem, recv_sem=recv_sem,
                device_id=device, device_id_type=MESH,
            ).start()
            return carry

        lax.fori_loop(1, PEERS, send, 0)

    def await_rows(target, rows, sem):
        some = target.at[pl.ds(0, (PEERS - 1) * rows)]
        pltpu.make_async_copy(some, some, sem).wait()

    def gather(target, units):
        return jnp.concatenate(
            [target[pl.ds(unit, PEERS, stride=BLOCK), :] for unit in units], axis=0
        )

    def weights(index):
        return table[index, 0], table[index, 1]

    def unit(x, part, line):
        return x * 8 + part * LINES + line

    def spectra(j, planes):
        partner = received[j, planes]
        count = partner.shape[0]
        field = jnp.concatenate(
            [(own[c, planes] * partner).reshape(count * N, N) for c in range(2)], axis=1
        )
        lines = product(split(field), weights(0))
        stacked = jnp.concatenate(
            [
                jnp.concatenate(
                    [lines[x * N : (x + 1) * N, c * N : (c + 1) * N] for x in range(count)], axis=1
                )
                for c in range(2)
            ],
            axis=0,
        )
        result = product(weights(1), split(stacked)).reshape(PEERS, 8, count * N)
        for i in range(count):
            x = planes.start + i
            out_a[j, :, x * 8 : (x + 1) * 8, :] = result[:, :, i * N : (i + 1) * N]

    def send_spectra(j, planes):
        rows = pl.ds(planes.start * 8, (planes.stop - planes.start) * 8)
        first = planes.start * 8
        size = (planes.stop - planes.start) * 8
        exchange(
            lambda to: out_a.at[j, to, rows],
            lambda me: in_a.at[j, pl.ds(me * BLOCK + first, size)],
            a_send.at[j], a_recv.at[j],
        )

    def keep(j, target, block):
        target[j, pl.ds(pl.multiple_of(grid * BLOCK, BLOCK), BLOCK), :] = block

    for x in range(LINES):
        for c in range(2):
            await_copy(own.at[c, x], own_recv.at[c, x])
        await_copy(received.at[0, x], received_recv.at[0, x])
        spectra(0, slice(x, x + 1))
        send_spectra(0, slice(x, x + 1))
    keep(0, in_a, out_a[0, grid])
    for x in range(LINES):
        await_copy(received.at[1, x], received_recv.at[1, x])
    spectra(1, slice(0, LINES))
    send_spectra(1, slice(0, LINES))
    keep(1, in_a, out_a[1, grid])

    def filtered(j):
        gathered = jnp.concatenate(
            [
                gather(
                    in_a.at[j],
                    [unit(x, part, line) for x in range(LINES) for part in range(2)],
                )
                for line in range(LINES)
            ],
            axis=1,
        )
        spectrum = product(weights(2), split(gathered))
        values = filt[...]
        spectrum = jnp.concatenate([spectrum[:N] * values, spectrum[N:] * values], axis=0)
        result = product(weights(3), split(spectrum))
        target = out_b.at[j]
        for x in range(LINES):
            for part in range(2):
                first = (x * 2 + part) * PEERS
                for line in range(LINES):
                    target[pl.ds(unit(x, part, line), PEERS, stride=BLOCK), :] = result[
                        first : first + PEERS, line * N : (line + 1) * N
                    ]

    def send_filtered(j, x, count, sem):
        size = count * 8
        exchange(
            lambda to: out_b.at[j, pl.ds(to * BLOCK + x * 8, size)],
            lambda me: in_b.at[j, pl.ds(me * BLOCK + x * 8, size)],
            b_send.at[sem], b_recv.at[sem],
        )

    for j in range(2):
        await_rows(in_a.at[j], BLOCK, a_recv.at[j])
        filtered(j)
        if j == 0:
            send_filtered(j, 0, LINES, 0)
        else:
            for x in range(LINES):
                send_filtered(j, x, 1, 1 + x)
        keep(j, in_b, out_b[j, pl.ds(pl.multiple_of(grid * BLOCK, BLOCK), BLOCK), :])

    def finish(j, x):
        gathered = gather(
            in_b.at[j],
            [unit(x, part, line) for line in range(LINES) for part in range(2)],
        )
        plane = product(weights(4), split(gathered))
        plane = jnp.concatenate([plane[:N], plane[N:]], axis=1)
        potential = product(split(plane), weights(5))
        parts = [potential[:, c * N : (c + 1) * N] for c in range(2)]
        back[j, x] = parts[0] * own[0, x] + parts[1] * own[1, x]
        for c in range(2):
            term = parts[c] * received[j, x]
            total[c, x] = term if j == 0 else total[c, x] + term

        @pl.when(lower)
        def _():
            pass_on(back.at[j, x], returned_hbm.at[j, x], ret_send.at[0], ret_recv.at[0], around(-1))
            if j == 1:
                for c in range(2):
                    stay(total.at[c, x], kept_hbm.at[c, x], kept_recv.at[0])

        if j == 1:

            @pl.when(upper == 1)
            def _():
                for c in range(2):
                    pass_on(
                        total.at[c, x], returned_hbm.at[c, x], ret_send.at[0], ret_recv.at[0], partner
                    )

        @pl.when(upper_even)
        def _():
            stay(back.at[j, x], kept_hbm.at[j, x], kept_recv.at[0])

        @pl.when(upper_odd)
        def _():
            pass_on(back.at[j, x], kept_hbm.at[j, x], kept_send.at[0], kept_recv.at[0], around(-2))

    await_rows(in_b.at[0], BLOCK, b_recv.at[0])
    for x in range(LINES):
        finish(0, x)
    for x in range(LINES):
        await_rows(in_b.at[1], 8, b_recv.at[1 + x])
        finish(1, x)

    await_copy(own, shift_send.at[0])
    for j in range(2):
        await_rows(in_a.at[j], BLOCK, a_send.at[j])
    await_rows(in_b.at[0], BLOCK, b_send.at[0])
    for x in range(LINES):
        await_rows(in_b.at[1], 8, b_send.at[1 + x])

    @pl.when(upper_odd)
    def _():
        await_copy(own, lent_send.at[0])
        await_copy(back, kept_send.at[0])

    await_copy(back, ret_send.at[0])
    await_copy(kept_hbm, kept_recv.at[0])
    await_copy(returned_hbm, ret_recv.at[0])


def per_device(orbitals, table):
    slab = (2, LINES, N, N)
    block = (2, PEERS, BLOCK, N)
    flat = (2, PEERS * BLOCK, N)
    f32 = jnp.float32
    dma = pltpu.SemaphoreType.DMA
    kept, returned = pl.pallas_call(
        kernel,
        out_shape=[jax.ShapeDtypeStruct(slab, f32)] * 2,
        in_specs=[pl.BlockSpec(memory_space=pltpu.HBM)] * 2,
        out_specs=[pl.BlockSpec(memory_space=pltpu.HBM)] * 2,
        scratch_shapes=[
            pltpu.VMEM(slab, f32),
            pltpu.VMEM(table.shape, f32),
            pltpu.VMEM((table.shape[0], 2, 2 * N, 2 * N), jnp.bfloat16),
            pltpu.VMEM(slab, f32),
            pltpu.VMEM((N, LINES * N), f32),
            pltpu.VMEM(block, f32),
            pltpu.VMEM(flat, f32),
            pltpu.VMEM(flat, f32),
            pltpu.VMEM(flat, f32),
            pltpu.VMEM(slab, f32),
            pltpu.VMEM(slab, f32),
            dma((1,)),
            dma((2, LINES)),
            dma((2, LINES)),
            dma((1,)),
            dma((1,)),
            dma((2,)),
            dma((2,)),
            dma((1 + LINES,)),
            dma((1 + LINES,)),
            dma((1,)),
            dma((1,)),
            dma((1,)),
            dma((1,)),
        ],
        compiler_params=pltpu.CompilerParams(
            collective_id=0, has_side_effects=True, vmem_limit_bytes=int(52.65 * 2**20)
        ),
    )(orbitals, table)
    return kept + returned


def solution(mesh):
    body = jax.shard_map(
        per_device,
        mesh=mesh,
        in_specs=(P("band", "grid", None, None), P()),
        out_specs=P("band", "grid", None, None),
        check_vma=False,
    )
    constants = tables()
    return lambda orbitals: body(orbitals, jnp.asarray(constants))
```

```python
import functools
import math

import jax
import jax.numpy as jnp
import numpy as np
from jax import lax
from jax.experimental import pallas as pl
from jax.experimental.pallas import tpu as pltpu
from jax.sharding import PartitionSpec as P

screening = 0.0428
MESH = pl.DeviceIdType.MESH
N = 128
LINES = 4
PEERS = 32
BANDS = 8
BLOCK = 8 * LINES


def complex_matrix(sign):
    points = np.arange(N)
    angle = (points[:, None] * points[None, :] % N) * (2.0 * math.pi / N)
    cosine, sine = np.cos(angle), sign * np.sin(angle)
    return np.block([[cosine, -sine], [sine, cosine]])


def peer_major():
    peer, part, line = np.meshgrid(np.arange(PEERS), np.arange(2), np.arange(LINES), indexing="ij")
    return (part * N + peer * LINES + line).reshape(-1)


def line_major():
    line, part, peer = np.meshgrid(np.arange(LINES), np.arange(2), np.arange(PEERS), indexing="ij")
    return (part * N + peer * LINES + line).reshape(-1)


def tables():
    forward, inverse = complex_matrix(-1), complex_matrix(1)
    peers, lines = peer_major(), line_major()
    return np.stack(
        [
            forward.T,
            forward[peers],
            forward[:, lines],
            inverse[lines],
            inverse[:, lines],
            inverse.T,
        ]
    ).astype(np.float32)


def split(x):
    high = x.astype(jnp.bfloat16)
    return high, (x - high.astype(jnp.float32)).astype(jnp.bfloat16)


def product(a, b):
    dot = functools.partial(jnp.dot, preferred_element_type=jnp.float32)
    return dot(a[0], b[0]) + (dot(a[0], b[1]) + dot(a[1], b[0]))


def signed(index):
    return jnp.where(index < N // 2, index, index - N).astype(jnp.float32) * (2.0 * math.pi / N)


def filter_values(me):
    shape = (N, LINES * N)
    lane = lax.broadcasted_iota(jnp.int32, shape, 1)
    kx = signed(lax.broadcasted_iota(jnp.int32, shape, 0))
    ky = signed(me * LINES + lane // N)
    kz = signed(lane % N)
    square = kx * kx + ky * ky + kz * kz
    positive = square > 0
    safe = jnp.where(positive, square, 1.0)
    value = 4.0 * math.pi * (1.0 - jnp.exp(-safe / (4.0 * screening * screening))) / safe
    value = jnp.where(positive, value, math.pi / (screening * screening))
    return value * (-0.25 / float(N * N * N))


def kernel(
    orb_hbm, table_hbm, kept_hbm, returned_hbm,
    home, own, exact, table, received, filt, out_a, in_a, out_b, in_b, back, total,
    table_sem, own_recv, received_recv, shift_send, lent_send,
    a_send, a_recv, b_send, b_recv, ret_send, ret_recv, kept_send, kept_recv,
):
    grid, band = lax.axis_index("grid"), lax.axis_index("band")
    upper, odd = lax.div(grid, PEERS // 2), lax.rem(band, 2)
    partner = band + 1 - 2 * odd
    lower = upper == 0
    upper_even = upper * (1 - odd) == 1
    upper_odd = upper * odd == 1

    def around(by):
        return lax.rem(band + (by + BANDS) % BANDS, BANDS)

    def peer(k):
        to = lax.rem(grid + k, PEERS)
        crosses = lax.rem(lax.div(to, PEERS // 2) + upper, 2)
        return to, {"band": band + crosses * (partner - band), "grid": to}

    load_home = pltpu.make_async_copy(orb_hbm, home, table_sem.at[1])
    load_home.start()
    load_table = pltpu.make_async_copy(table_hbm, exact, table_sem.at[0])
    load_table.start()

    barrier = pltpu.get_barrier_semaphore()

    def greet_band(to):
        pl.semaphore_signal(barrier, inc=1, device_id={"band": to}, device_id_type=MESH)

    @pl.when(lower)
    def _():
        greet_band(around(1))
        greet_band(around(-1))

    @pl.when(upper == 1)
    def _():
        greet_band(partner)

    @pl.when(upper_odd)
    def _():
        greet_band(around(2))
        greet_band(around(-2))

    def greet(k, carry):
        pl.semaphore_signal(barrier, inc=1, device_id=peer(k)[1], device_id_type=MESH)
        return carry

    lax.fori_loop(1, PEERS, greet, 0)
    pl.semaphore_wait(barrier, PEERS - 1 + (1 - upper) * 2 + upper * (1 + 2 * odd))

    load_home.wait()

    def pass_on(source, target, send_sem, recv_sem, to):
        pltpu.make_async_remote_copy(
            src_ref=source, dst_ref=target, send_sem=send_sem, recv_sem=recv_sem,
            device_id={"band": to}, device_id_type=MESH,
        ).start()

    def stay(source, target, sem):
        pltpu.make_async_copy(source, target, sem).start()

    def await_copy(ref, sem):
        pltpu.make_async_copy(ref, ref, sem).wait()

    pairs = [(c, x) for x in range(LINES) for c in range(2)]
    slabs = [(j, x) for j in range(2) for x in range(LINES)]

    @pl.when(lower)
    def _():
        for j, x in slabs:
            pass_on(
                home.at[j, x], received.at[j, x], shift_send.at[0], received_recv.at[j, x], around(1)
            )
        for c, x in pairs:
            stay(home.at[c, x], own.at[c, x], own_recv.at[c, x])

    @pl.when(upper == 1)
    def _():
        for c, x in pairs:
            pass_on(home.at[c, x], own.at[c, x], shift_send.at[0], own_recv.at[c, x], partner)

    @pl.when(upper_even)
    def _():
        for j, x in slabs:
            stay(home.at[j, x], received.at[j, x], received_recv.at[j, x])

    @pl.when(upper_odd)
    def _():
        for j, x in slabs:
            pass_on(
                home.at[j, x], received.at[j, x], lent_send.at[0], received_recv.at[j, x], around(2)
            )

    filt[...] = filter_values(grid)
    load_table.wait()
    for index in range(6):
        table[index, 0], table[index, 1] = split(exact[index])

    def exchange(source, target, send_sem, recv_sem, by_core=False):
        def send(to, device):
            pltpu.make_async_remote_copy(
                src_ref=source(to), dst_ref=target(grid),
                send_sem=send_sem, recv_sem=recv_sem,
                device_id=device, device_id_type=MESH,
            ).start()

        def next_peer(k, carry):
            send(*peer(k))
            return carry

        def next_chip(i, core):
            chip = lax.rem(lax.div(grid, 2) + i, PEERS // 2)
            to = chip * 2 + core
            crosses = lax.rem(lax.div(chip, PEERS // 4) + upper, 2)

            @pl.when(to != grid)
            def _():
                send(to, {"band": band + crosses * (partner - band), "grid": to})

            return core

        if by_core:
            for core in range(2):
                lax.fori_loop(0, PEERS // 2, next_chip, core)
        else:
            lax.fori_loop(1, PEERS, next_peer, 0)

    def await_rows(target, rows, sem):
        some = target.at[pl.ds(0, (PEERS - 1) * rows)]
        pltpu.make_async_copy(some, some, sem).wait()

    def gather(target, units):
        return jnp.concatenate(
            [target[pl.ds(unit, PEERS, stride=BLOCK), :] for unit in units], axis=0
        )

    def weights(index):
        return table[index, 0], table[index, 1]

    def unit(x, part, line):
        return x * 8 + part * LINES + line

    def spectra(j, planes):
        partner = received[j, planes]
        count = partner.shape[0]
        field = jnp.concatenate(
            [(own[c, planes] * partner).reshape(count * N, N) for c in range(2)], axis=1
        )
        lines = product(split(field), weights(0))
        stacked = jnp.concatenate(
            [
                jnp.concatenate(
                    [lines[x * N : (x + 1) * N, c * N : (c + 1) * N] for x in range(count)], axis=1
                )
                for c in range(2)
            ],
            axis=0,
        )
        result = product(weights(1), split(stacked)).reshape(PEERS, 8, count * N)
        for i in range(count):
            x = planes.start + i
            out_a[j, :, x * 8 : (x + 1) * 8, :] = result[:, :, i * N : (i + 1) * N]

    def send_spectra(j, planes):
        rows = pl.ds(planes.start * 8, (planes.stop - planes.start) * 8)
        first = planes.start * 8
        size = (planes.stop - planes.start) * 8
        exchange(
            lambda to: out_a.at[j, to, rows],
            lambda me: in_a.at[j, pl.ds(me * BLOCK + first, size)],
            a_send.at[j], a_recv.at[j],
        )

    def keep(j, target, block):
        target[j, pl.ds(pl.multiple_of(grid * BLOCK, BLOCK), BLOCK), :] = block

    for x in range(LINES):
        for c in range(2):
            await_copy(own.at[c, x], own_recv.at[c, x])
        await_copy(received.at[0, x], received_recv.at[0, x])
        spectra(0, slice(x, x + 1))
        send_spectra(0, slice(x, x + 1))
    keep(0, in_a, out_a[0, grid])
    for x in range(LINES):
        await_copy(received.at[1, x], received_recv.at[1, x])
    spectra(1, slice(0, LINES))
    send_spectra(1, slice(0, LINES))
    keep(1, in_a, out_a[1, grid])

    def filtered(j):
        gathered = jnp.concatenate(
            [
                gather(
                    in_a.at[j],
                    [unit(x, part, line) for x in range(LINES) for part in range(2)],
                )
                for line in range(LINES)
            ],
            axis=1,
        )
        spectrum = product(weights(2), split(gathered))
        values = filt[...]
        spectrum = jnp.concatenate([spectrum[:N] * values, spectrum[N:] * values], axis=0)
        result = product(weights(3), split(spectrum))
        target = out_b.at[j]
        for x in range(LINES):
            for part in range(2):
                first = (x * 2 + part) * PEERS
                for line in range(LINES):
                    target[pl.ds(unit(x, part, line), PEERS, stride=BLOCK), :] = result[
                        first : first + PEERS, line * N : (line + 1) * N
                    ]

    def send_filtered(j, x, count, sem):
        size = count * 8
        exchange(
            lambda to: out_b.at[j, pl.ds(to * BLOCK + x * 8, size)],
            lambda me: in_b.at[j, pl.ds(me * BLOCK + x * 8, size)],
            b_send.at[sem], b_recv.at[sem], sem > 0,
        )

    for j in range(2):
        await_rows(in_a.at[j], BLOCK, a_recv.at[j])
        filtered(j)
        if j == 0:
            send_filtered(j, 0, LINES, 0)
        else:
            for x in range(LINES):
                send_filtered(j, x, 1, 1 + x)
        keep(j, in_b, out_b[j, pl.ds(pl.multiple_of(grid * BLOCK, BLOCK), BLOCK), :])

    def finish(j, x):
        gathered = gather(
            in_b.at[j],
            [unit(x, part, line) for line in range(LINES) for part in range(2)],
        )
        plane = product(weights(4), split(gathered))
        plane = jnp.concatenate([plane[:N], plane[N:]], axis=1)
        potential = product(split(plane), weights(5))
        parts = [potential[:, c * N : (c + 1) * N] for c in range(2)]
        back[j, x] = parts[0] * own[0, x] + parts[1] * own[1, x]
        for c in range(2):
            term = parts[c] * received[j, x]
            total[c, x] = term if j == 0 else total[c, x] + term

        @pl.when(lower)
        def _():
            pass_on(back.at[j, x], returned_hbm.at[j, x], ret_send.at[0], ret_recv.at[0], around(-1))
            if j == 1:
                for c in range(2):
                    stay(total.at[c, x], kept_hbm.at[c, x], kept_recv.at[0])

        if j == 1:

            @pl.when(upper == 1)
            def _():
                for c in range(2):
                    pass_on(
                        total.at[c, x], returned_hbm.at[c, x], ret_send.at[0], ret_recv.at[0], partner
                    )

        @pl.when(upper_even)
        def _():
            stay(back.at[j, x], kept_hbm.at[j, x], kept_recv.at[0])

        @pl.when(upper_odd)
        def _():
            pass_on(back.at[j, x], kept_hbm.at[j, x], kept_send.at[0], kept_recv.at[0], around(-2))

    await_rows(in_b.at[0], BLOCK, b_recv.at[0])
    for x in range(LINES):
        finish(0, x)
    for x in range(LINES):
        await_rows(in_b.at[1], 8, b_recv.at[1 + x])
        finish(1, x)

    await_copy(own, shift_send.at[0])
    for j in range(2):
        await_rows(in_a.at[j], BLOCK, a_send.at[j])
    await_rows(in_b.at[0], BLOCK, b_send.at[0])
    for x in range(LINES):
        await_rows(in_b.at[1], 8, b_send.at[1 + x])

    @pl.when(upper_odd)
    def _():
        await_copy(own, lent_send.at[0])
        await_copy(back, kept_send.at[0])

    await_copy(back, ret_send.at[0])
    await_copy(kept_hbm, kept_recv.at[0])
    await_copy(returned_hbm, ret_recv.at[0])


def per_device(orbitals, table):
    slab = (2, LINES, N, N)
    block = (2, PEERS, BLOCK, N)
    flat = (2, PEERS * BLOCK, N)
    f32 = jnp.float32
    dma = pltpu.SemaphoreType.DMA
    kept, returned = pl.pallas_call(
        kernel,
        out_shape=[jax.ShapeDtypeStruct(slab, f32)] * 2,
        in_specs=[pl.BlockSpec(memory_space=pltpu.HBM)] * 2,
        out_specs=[pl.BlockSpec(memory_space=pltpu.HBM)] * 2,
        scratch_shapes=[
            pltpu.VMEM(slab, f32),
            pltpu.VMEM(slab, f32),
            pltpu.VMEM(table.shape, f32),
            pltpu.VMEM((table.shape[0], 2, 2 * N, 2 * N), jnp.bfloat16),
            pltpu.VMEM(slab, f32),
            pltpu.VMEM((N, LINES * N), f32),
            pltpu.VMEM(block, f32),
            pltpu.VMEM(flat, f32),
            pltpu.VMEM(flat, f32),
            pltpu.VMEM(flat, f32),
            pltpu.VMEM(slab, f32),
            pltpu.VMEM(slab, f32),
            dma((2,)),
            dma((2, LINES)),
            dma((2, LINES)),
            dma((1,)),
            dma((1,)),
            dma((2,)),
            dma((2,)),
            dma((1 + LINES,)),
            dma((1 + LINES,)),
            dma((1,)),
            dma((1,)),
            dma((1,)),
            dma((1,)),
        ],
        compiler_params=pltpu.CompilerParams(
            collective_id=0, has_side_effects=True, vmem_limit_bytes=int(52.65 * 2**20)
        ),
    )(orbitals, table)
    return kept + returned


def solution(mesh):
    body = jax.shard_map(
        per_device,
        mesh=mesh,
        in_specs=(P("band", "grid", None, None), P()),
        out_specs=P("band", "grid", None, None),
        check_vma=False,
    )
    constants = tables()
    return lambda orbitals: body(orbitals, jnp.asarray(constants))
```

```python
import functools
import math

import jax
import jax.numpy as jnp
import numpy as np
from jax import lax
from jax.experimental import pallas as pl
from jax.experimental.pallas import tpu as pltpu
from jax.sharding import PartitionSpec as P

screening = 0.0428
MESH = pl.DeviceIdType.MESH
N = 128
LINES = 4
PEERS = 32
BANDS = 8
BLOCK = 8 * LINES


def complex_matrix(sign):
    points = np.arange(N)
    angle = (points[:, None] * points[None, :] % N) * (2.0 * math.pi / N)
    cosine, sine = np.cos(angle), sign * np.sin(angle)
    return np.block([[cosine, -sine], [sine, cosine]])


def peer_major():
    peer, part, line = np.meshgrid(np.arange(PEERS), np.arange(2), np.arange(LINES), indexing="ij")
    return (part * N + peer * LINES + line).reshape(-1)


def line_major():
    line, part, peer = np.meshgrid(np.arange(LINES), np.arange(2), np.arange(PEERS), indexing="ij")
    return (part * N + peer * LINES + line).reshape(-1)


def tables():
    forward, inverse = complex_matrix(-1), complex_matrix(1)
    peers, lines = peer_major(), line_major()
    return np.stack(
        [
            forward.T,
            forward[peers],
            forward[:, lines],
            inverse[lines],
            inverse[:, lines],
            inverse.T,
        ]
    ).astype(np.float32)


def split(x):
    high = x.astype(jnp.bfloat16)
    return high, (x - high.astype(jnp.float32)).astype(jnp.bfloat16)


def product(a, b):
    dot = functools.partial(jnp.dot, preferred_element_type=jnp.float32)
    return dot(a[0], b[0]) + (dot(a[0], b[1]) + dot(a[1], b[0]))


def signed(index):
    return jnp.where(index < N // 2, index, index - N).astype(jnp.float32) * (2.0 * math.pi / N)


def filter_values(me):
    shape = (N, LINES * N)
    lane = lax.broadcasted_iota(jnp.int32, shape, 1)
    kx = signed(lax.broadcasted_iota(jnp.int32, shape, 0))
    ky = signed(me * LINES + lane // N)
    kz = signed(lane % N)
    square = kx * kx + ky * ky + kz * kz
    positive = square > 0
    safe = jnp.where(positive, square, 1.0)
    value = 4.0 * math.pi * (1.0 - jnp.exp(-safe / (4.0 * screening * screening))) / safe
    value = jnp.where(positive, value, math.pi / (screening * screening))
    return value * (-0.25 / float(N * N * N))


def kernel(
    orb_hbm, table_hbm, kept_hbm, returned_hbm,
    home, own, exact, table, received, filt, out_a, in_a, out_b, in_b, back, total,
    table_sem, own_recv, received_recv, shift_send, lent_send,
    a_send, a_recv, b_send, b_recv, ret_send, ret_recv, kept_send, kept_recv,
):
    grid, band = lax.axis_index("grid"), lax.axis_index("band")
    upper, odd = lax.div(grid, PEERS // 2), lax.rem(band, 2)
    partner = band + 1 - 2 * odd
    lower = upper == 0
    lower_band = band + upper * (partner - band)
    upper_band = band + (1 - upper) * (partner - band)
    upper_even = upper * (1 - odd) == 1
    upper_odd = upper * odd == 1

    def around(by):
        return lax.rem(band + (by + BANDS) % BANDS, BANDS)

    def peer(k):
        to = grid + k
        to = jnp.where(to >= PEERS, to - PEERS, to)
        return to, {"band": jnp.where(to >= PEERS // 2, upper_band, lower_band), "grid": to}

    load_home = pltpu.make_async_copy(orb_hbm, home, table_sem.at[1])
    load_home.start()
    load_table = pltpu.make_async_copy(table_hbm, exact, table_sem.at[0])
    load_table.start()

    barrier = pltpu.get_barrier_semaphore()

    def greet_band(to):
        pl.semaphore_signal(barrier, inc=1, device_id={"band": to}, device_id_type=MESH)

    @pl.when(lower)
    def _():
        greet_band(around(1))
        greet_band(around(-1))

    @pl.when(upper == 1)
    def _():
        greet_band(partner)

    @pl.when(upper_odd)
    def _():
        greet_band(around(2))
        greet_band(around(-2))

    def greet(k, carry):
        pl.semaphore_signal(barrier, inc=1, device_id=peer(k)[1], device_id_type=MESH)
        return carry

    lax.fori_loop(1, PEERS, greet, 0)
    pl.semaphore_wait(barrier, PEERS - 1 + (1 - upper) * 2 + upper * (1 + 2 * odd))

    load_home.wait()

    def pass_on(source, target, send_sem, recv_sem, to):
        pltpu.make_async_remote_copy(
            src_ref=source, dst_ref=target, send_sem=send_sem, recv_sem=recv_sem,
            device_id={"band": to}, device_id_type=MESH,
        ).start()

    def stay(source, target, sem):
        pltpu.make_async_copy(source, target, sem).start()

    def await_copy(ref, sem):
        pltpu.make_async_copy(ref, ref, sem).wait()

    pairs = [(c, x) for x in range(LINES) for c in range(2)]
    slabs = [(j, x) for j in range(2) for x in range(LINES)]

    @pl.when(lower)
    def _():
        for j, x in slabs:
            pass_on(
                home.at[j, x], received.at[j, x], shift_send.at[0], received_recv.at[j, x], around(1)
            )
        for c, x in pairs:
            stay(home.at[c, x], own.at[c, x], own_recv.at[c, x])

    @pl.when(upper == 1)
    def _():
        for c, x in pairs:
            pass_on(home.at[c, x], own.at[c, x], shift_send.at[0], own_recv.at[c, x], partner)

    @pl.when(upper_even)
    def _():
        for j, x in slabs:
            stay(home.at[j, x], received.at[j, x], received_recv.at[j, x])

    @pl.when(upper_odd)
    def _():
        for j, x in slabs:
            pass_on(
                home.at[j, x], received.at[j, x], lent_send.at[0], received_recv.at[j, x], around(2)
            )

    def split_table(index):
        table[index, 0], table[index, 1] = split(exact[index])

    def prepare_return():
        filt[...] = filter_values(grid)
        for index in range(2, 6):
            split_table(index)

    load_table.wait()
    split_table(0)
    split_table(1)

    def exchange(source, target, send_sem, recv_sem, by_core=False):
        def send(to, device):
            pltpu.make_async_remote_copy(
                src_ref=source(to), dst_ref=target(grid),
                send_sem=send_sem, recv_sem=recv_sem,
                device_id=device, device_id_type=MESH,
            ).start()

        def next_peer(k, carry):
            send(*peer(k))
            return carry

        def next_chip(i, core):
            chip = lax.div(grid, 2) + i
            chip = jnp.where(chip >= PEERS // 2, chip - PEERS // 2, chip)
            to = chip * 2 + core

            @pl.when(to != grid)
            def _():
                group = jnp.where(chip >= PEERS // 4, upper_band, lower_band)
                send(to, {"band": group, "grid": to})

            return core

        if by_core:
            for core in range(2):
                lax.fori_loop(0, PEERS // 2, next_chip, core)
        else:
            lax.fori_loop(1, PEERS, next_peer, 0)

    def await_rows(target, rows, sem):
        some = target.at[pl.ds(0, (PEERS - 1) * rows)]
        pltpu.make_async_copy(some, some, sem).wait()

    def gather(target, units):
        return jnp.concatenate(
            [target[pl.ds(unit, PEERS, stride=BLOCK), :] for unit in units], axis=0
        )

    def weights(index):
        return table[index, 0], table[index, 1]

    def unit(x, part, line):
        return x * 8 + part * LINES + line

    def spectra(j, planes):
        partner = received[j, planes]
        count = partner.shape[0]
        field = jnp.concatenate(
            [(own[c, planes] * partner).reshape(count * N, N) for c in range(2)], axis=1
        )
        lines = product(split(field), weights(0))
        stacked = jnp.concatenate(
            [
                jnp.concatenate(
                    [lines[x * N : (x + 1) * N, c * N : (c + 1) * N] for x in range(count)], axis=1
                )
                for c in range(2)
            ],
            axis=0,
        )
        result = product(weights(1), split(stacked)).reshape(PEERS, 8, count * N)
        for i in range(count):
            x = planes.start + i
            out_a[j, :, x * 8 : (x + 1) * 8, :] = result[:, :, i * N : (i + 1) * N]

    def send_spectra(j, planes):
        rows = pl.ds(planes.start * 8, (planes.stop - planes.start) * 8)
        first = planes.start * 8
        size = (planes.stop - planes.start) * 8
        exchange(
            lambda to: out_a.at[j, to, rows],
            lambda me: in_a.at[j, pl.ds(me * BLOCK + first, size)],
            a_send.at[j], a_recv.at[j],
        )

    def keep(j, target, block):
        target[j, pl.ds(pl.multiple_of(grid * BLOCK, BLOCK), BLOCK), :] = block

    for x in range(LINES):
        for c in range(2):
            await_copy(own.at[c, x], own_recv.at[c, x])
        await_copy(received.at[0, x], received_recv.at[0, x])
        spectra(0, slice(x, x + 1))
        send_spectra(0, slice(x, x + 1))
    keep(0, in_a, out_a[0, grid])
    for x in range(LINES):
        await_copy(received.at[1, x], received_recv.at[1, x])
    spectra(1, slice(0, LINES))
    send_spectra(1, slice(0, LINES))
    keep(1, in_a, out_a[1, grid])
    prepare_return()

    def filtered(j):
        gathered = jnp.concatenate(
            [
                gather(
                    in_a.at[j],
                    [unit(x, part, line) for x in range(LINES) for part in range(2)],
                )
                for line in range(LINES)
            ],
            axis=1,
        )
        spectrum = product(weights(2), split(gathered))
        values = filt[...]
        spectrum = jnp.concatenate([spectrum[:N] * values, spectrum[N:] * values], axis=0)
        result = product(weights(3), split(spectrum))
        target = out_b.at[j]
        for x in range(LINES):
            for part in range(2):
                first = (x * 2 + part) * PEERS
                for line in range(LINES):
                    target[pl.ds(unit(x, part, line), PEERS, stride=BLOCK), :] = result[
                        first : first + PEERS, line * N : (line + 1) * N
                    ]

    def send_filtered(j, x, count, sem):
        size = count * 8
        exchange(
            lambda to: out_b.at[j, pl.ds(to * BLOCK + x * 8, size)],
            lambda me: in_b.at[j, pl.ds(me * BLOCK + x * 8, size)],
            b_send.at[sem], b_recv.at[sem], sem > 0,
        )

    for j in range(2):
        await_rows(in_a.at[j], BLOCK, a_recv.at[j])
        filtered(j)
        if j == 0:
            send_filtered(j, 0, LINES, 0)
        else:
            for x in range(LINES):
                send_filtered(j, x, 1, 1 + x)
        keep(j, in_b, out_b[j, pl.ds(pl.multiple_of(grid * BLOCK, BLOCK), BLOCK), :])

    def finish(j, x):
        gathered = gather(
            in_b.at[j],
            [unit(x, part, line) for line in range(LINES) for part in range(2)],
        )
        plane = product(weights(4), split(gathered))
        plane = jnp.concatenate([plane[:N], plane[N:]], axis=1)
        potential = product(split(plane), weights(5))
        parts = [potential[:, c * N : (c + 1) * N] for c in range(2)]
        back[j, x] = parts[0] * own[0, x] + parts[1] * own[1, x]
        for c in range(2):
            term = parts[c] * received[j, x]
            total[c, x] = term if j == 0 else total[c, x] + term

        @pl.when(lower)
        def _():
            pass_on(back.at[j, x], returned_hbm.at[j, x], ret_send.at[0], ret_recv.at[0], around(-1))
            if j == 1:
                for c in range(2):
                    stay(total.at[c, x], kept_hbm.at[c, x], kept_recv.at[0])

        if j == 1:

            @pl.when(upper == 1)
            def _():
                for c in range(2):
                    pass_on(
                        total.at[c, x], returned_hbm.at[c, x], ret_send.at[0], ret_recv.at[0], partner
                    )

        @pl.when(upper_even)
        def _():
            stay(back.at[j, x], kept_hbm.at[j, x], kept_recv.at[0])

        @pl.when(upper_odd)
        def _():
            pass_on(back.at[j, x], kept_hbm.at[j, x], kept_send.at[0], kept_recv.at[0], around(-2))

    await_rows(in_b.at[0], BLOCK, b_recv.at[0])
    for x in range(LINES):
        finish(0, x)
    for x in range(LINES):
        await_rows(in_b.at[1], 8, b_recv.at[1 + x])
        finish(1, x)

    await_copy(own, shift_send.at[0])
    for j in range(2):
        await_rows(in_a.at[j], BLOCK, a_send.at[j])
    await_rows(in_b.at[0], BLOCK, b_send.at[0])
    for x in range(LINES):
        await_rows(in_b.at[1], 8, b_send.at[1 + x])

    @pl.when(upper_odd)
    def _():
        await_copy(own, lent_send.at[0])
        await_copy(back, kept_send.at[0])

    await_copy(back, ret_send.at[0])
    await_copy(kept_hbm, kept_recv.at[0])
    await_copy(returned_hbm, ret_recv.at[0])


def per_device(orbitals, table):
    slab = (2, LINES, N, N)
    block = (2, PEERS, BLOCK, N)
    flat = (2, PEERS * BLOCK, N)
    f32 = jnp.float32
    dma = pltpu.SemaphoreType.DMA
    kept, returned = pl.pallas_call(
        kernel,
        out_shape=[jax.ShapeDtypeStruct(slab, f32)] * 2,
        in_specs=[pl.BlockSpec(memory_space=pltpu.HBM)] * 2,
        out_specs=[pl.BlockSpec(memory_space=pltpu.HBM)] * 2,
        scratch_shapes=[
            pltpu.VMEM(slab, f32),
            pltpu.VMEM(slab, f32),
            pltpu.VMEM(table.shape, f32),
            pltpu.VMEM((table.shape[0], 2, 2 * N, 2 * N), jnp.bfloat16),
            pltpu.VMEM(slab, f32),
            pltpu.VMEM((N, LINES * N), f32),
            pltpu.VMEM(block, f32),
            pltpu.VMEM(flat, f32),
            pltpu.VMEM(flat, f32),
            pltpu.VMEM(flat, f32),
            pltpu.VMEM(slab, f32),
            pltpu.VMEM(slab, f32),
            dma((2,)),
            dma((2, LINES)),
            dma((2, LINES)),
            dma((1,)),
            dma((1,)),
            dma((2,)),
            dma((2,)),
            dma((1 + LINES,)),
            dma((1 + LINES,)),
            dma((1,)),
            dma((1,)),
            dma((1,)),
            dma((1,)),
        ],
        compiler_params=pltpu.CompilerParams(
            collective_id=0, has_side_effects=True, vmem_limit_bytes=int(52.65 * 2**20)
        ),
    )(orbitals, table)
    return kept + returned


def solution(mesh):
    body = jax.shard_map(
        per_device,
        mesh=mesh,
        in_specs=(P("band", "grid", None, None), P()),
        out_specs=P("band", "grid", None, None),
        check_vma=False,
    )
    constants = tables()
    return lambda orbitals: body(orbitals, jnp.asarray(constants))
```

```python
import functools
import math

import jax
import jax.numpy as jnp
import numpy as np
from jax import lax
from jax.experimental import pallas as pl
from jax.experimental.pallas import tpu as pltpu
from jax.sharding import PartitionSpec as P

screening = 0.0428
MESH = pl.DeviceIdType.MESH
N = 128
LINES = 4
PEERS = 32
BANDS = 8
BLOCK = 8 * LINES


def complex_matrix(sign):
    points = np.arange(N)
    angle = (points[:, None] * points[None, :] % N) * (2.0 * math.pi / N)
    cosine, sine = np.cos(angle), sign * np.sin(angle)
    return np.block([[cosine, -sine], [sine, cosine]])


def peer_major():
    peer, part, line = np.meshgrid(np.arange(PEERS), np.arange(2), np.arange(LINES), indexing="ij")
    return (part * N + peer * LINES + line).reshape(-1)


def line_major():
    line, part, peer = np.meshgrid(np.arange(LINES), np.arange(2), np.arange(PEERS), indexing="ij")
    return (part * N + peer * LINES + line).reshape(-1)


def tables():
    forward, inverse = complex_matrix(-1), complex_matrix(1)
    peers, lines = peer_major(), line_major()
    return np.stack(
        [
            forward.T,
            forward[peers],
            forward[:, lines],
            inverse[lines],
            inverse[:, lines],
            inverse.T,
        ]
    ).astype(np.float32)


def split(x):
    high = x.astype(jnp.bfloat16)
    return high, (x - high.astype(jnp.float32)).astype(jnp.bfloat16)


def product(a, b):
    dot = functools.partial(jnp.dot, preferred_element_type=jnp.float32)
    return dot(a[0], b[0]) + (dot(a[0], b[1]) + dot(a[1], b[0]))


def signed(index):
    return jnp.where(index < N // 2, index, index - N).astype(jnp.float32) * (2.0 * math.pi / N)


def filter_values(me):
    shape = (N, LINES * N)
    lane = lax.broadcasted_iota(jnp.int32, shape, 1)
    kx = signed(lax.broadcasted_iota(jnp.int32, shape, 0))
    ky = signed(me * LINES + lane // N)
    kz = signed(lane % N)
    square = kx * kx + ky * ky + kz * kz
    positive = square > 0
    safe = jnp.where(positive, square, 1.0)
    value = 4.0 * math.pi * (1.0 - jnp.exp(-safe / (4.0 * screening * screening))) / safe
    value = jnp.where(positive, value, math.pi / (screening * screening))
    return value * (-0.25 / float(N * N * N))


def kernel(
    orb_hbm, table_hbm, kept_hbm, returned_hbm,
    home, own, exact, table, received, filt, out_a, in_a, out_b, in_b, back, total,
    table_sem, own_recv, received_recv, shift_send, lent_send,
    a_send, a_recv, b_send, b_recv, ret_send, ret_recv, kept_send, kept_recv,
):
    grid, band = lax.axis_index("grid"), lax.axis_index("band")
    upper, odd = lax.div(grid, PEERS // 2), lax.rem(band, 2)
    partner = band + 1 - 2 * odd
    lower = upper == 0
    lower_band = band + upper * (partner - band)
    upper_band = band + (1 - upper) * (partner - band)
    upper_even = upper * (1 - odd) == 1
    upper_odd = upper * odd == 1

    def around(by):
        return lax.rem(band + (by + BANDS) % BANDS, BANDS)

    def peer(k):
        to = grid + k
        to = jnp.where(to >= PEERS, to - PEERS, to)
        return to, {"band": jnp.where(to >= PEERS // 2, upper_band, lower_band), "grid": to}

    load_home = pltpu.make_async_copy(orb_hbm, home, table_sem.at[1])
    load_home.start()
    load_table = pltpu.make_async_copy(table_hbm, exact, table_sem.at[0])
    load_table.start()

    barrier = pltpu.get_barrier_semaphore()

    def greet_band(to):
        pl.semaphore_signal(barrier, inc=1, device_id={"band": to}, device_id_type=MESH)

    @pl.when(lower)
    def _():
        greet_band(around(1))
        greet_band(around(-1))

    @pl.when(upper == 1)
    def _():
        greet_band(partner)

    @pl.when(upper_odd)
    def _():
        greet_band(around(2))
        greet_band(around(-2))

    def greet(k, carry):
        pl.semaphore_signal(barrier, inc=1, device_id=peer(k)[1], device_id_type=MESH)
        return carry

    lax.fori_loop(1, PEERS, greet, 0)
    pl.semaphore_wait(barrier, PEERS - 1 + (1 - upper) * 2 + upper * (1 + 2 * odd))

    load_home.wait()

    def pass_on(source, target, send_sem, recv_sem, to):
        pltpu.make_async_remote_copy(
            src_ref=source, dst_ref=target, send_sem=send_sem, recv_sem=recv_sem,
            device_id={"band": to}, device_id_type=MESH,
        ).start()

    def stay(source, target, sem):
        pltpu.make_async_copy(source, target, sem).start()

    def await_copy(ref, sem):
        pltpu.make_async_copy(ref, ref, sem).wait()

    pairs = [(c, x) for x in range(LINES) for c in range(2)]
    slabs = [(j, x) for j in range(2) for x in range(LINES)]

    @pl.when(lower)
    def _():
        for j, x in slabs:
            pass_on(
                home.at[j, x], received.at[j, x], shift_send.at[0], received_recv.at[j, x], around(1)
            )
        for c, x in pairs:
            stay(home.at[c, x], own.at[c, x], own_recv.at[c, x])

    @pl.when(upper == 1)
    def _():
        for c, x in pairs:
            pass_on(home.at[c, x], own.at[c, x], shift_send.at[0], own_recv.at[c, x], partner)

    @pl.when(upper_even)
    def _():
        for j, x in slabs:
            stay(home.at[j, x], received.at[j, x], received_recv.at[j, x])

    @pl.when(upper_odd)
    def _():
        for j, x in slabs:
            pass_on(
                home.at[j, x], received.at[j, x], lent_send.at[0], received_recv.at[j, x], around(2)
            )

    def split_table(index):
        table[index, 0], table[index, 1] = split(exact[index])

    def prepare_return():
        filt[...] = filter_values(grid)
        for index in range(2, 6):
            split_table(index)

    load_table.wait()
    split_table(0)
    split_table(1)

    def exchange(source, target, send_sem, recv_sem, by_core=False):
        def send(to, device):
            pltpu.make_async_remote_copy(
                src_ref=source(to), dst_ref=target(grid),
                send_sem=send_sem, recv_sem=recv_sem,
                device_id=device, device_id_type=MESH,
            ).start()

        def next_peer(k, carry):
            send(*peer(k))
            return carry

        def next_chip(i, core):
            chip = lax.div(grid, 2) + i
            chip = jnp.where(chip >= PEERS // 2, chip - PEERS // 2, chip)
            to = chip * 2 + core

            @pl.when(to != grid)
            def _():
                group = jnp.where(chip >= PEERS // 4, upper_band, lower_band)
                send(to, {"band": group, "grid": to})

            return core

        if by_core:
            for core in range(2):
                lax.fori_loop(0, PEERS // 2, next_chip, core)
        else:
            lax.fori_loop(1, PEERS, next_peer, 0)

    def await_rows(target, rows, sem):
        some = target.at[pl.ds(0, (PEERS - 1) * rows)]
        pltpu.make_async_copy(some, some, sem).wait()

    def gather(target, units):
        return jnp.concatenate(
            [target[pl.ds(unit, PEERS, stride=BLOCK), :] for unit in units], axis=0
        )

    def weights(index):
        return table[index, 0], table[index, 1]

    def unit(x, part, line):
        return x * 8 + part * LINES + line

    def spectra(j, planes):
        partner = received[j, planes]
        count = partner.shape[0]
        field = jnp.concatenate(
            [(own[c, planes] * partner).reshape(count * N, N) for c in range(2)], axis=1
        )
        lines = product(split(field), weights(0))
        stacked = jnp.concatenate(
            [
                jnp.concatenate(
                    [lines[x * N : (x + 1) * N, c * N : (c + 1) * N] for x in range(count)], axis=1
                )
                for c in range(2)
            ],
            axis=0,
        )
        result = product(weights(1), split(stacked)).reshape(PEERS, 8, count * N)
        for i in range(count):
            x = planes.start + i
            out_a[j, :, x * 8 : (x + 1) * 8, :] = result[:, :, i * N : (i + 1) * N]

    def send_spectra(j, planes):
        rows = pl.ds(planes.start * 8, (planes.stop - planes.start) * 8)
        first = planes.start * 8
        size = (planes.stop - planes.start) * 8
        exchange(
            lambda to: out_a.at[j, to, rows],
            lambda me: in_a.at[j, pl.ds(me * BLOCK + first, size)],
            a_send.at[j], a_recv.at[j],
        )

    def keep(j, target, block):
        target[j, pl.ds(pl.multiple_of(grid * BLOCK, BLOCK), BLOCK), :] = block

    for x in range(LINES):
        for c in range(2):
            await_copy(own.at[c, x], own_recv.at[c, x])
        await_copy(received.at[0, x], received_recv.at[0, x])
        spectra(0, slice(x, x + 1))
        send_spectra(0, slice(x, x + 1))
    keep(0, in_a, out_a[0, grid])
    for x in range(LINES):
        await_copy(received.at[1, x], received_recv.at[1, x])
    spectra(1, slice(0, LINES))
    send_spectra(1, slice(0, LINES))
    keep(1, in_a, out_a[1, grid])
    prepare_return()

    def filtered(j):
        gathered = jnp.concatenate(
            [
                gather(
                    in_a.at[j],
                    [unit(x, part, line) for x in range(LINES) for part in range(2)],
                )
                for line in range(LINES)
            ],
            axis=1,
        )
        spectrum = product(weights(2), split(gathered))
        values = filt[...]
        spectrum = jnp.concatenate([spectrum[:N] * values, spectrum[N:] * values], axis=0)
        result = product(weights(3), split(spectrum))
        target = out_b.at[j]
        for x in range(LINES):
            for part in range(2):
                first = (x * 2 + part) * PEERS
                for line in range(LINES):
                    target[pl.ds(unit(x, part, line), PEERS, stride=BLOCK), :] = result[
                        first : first + PEERS, line * N : (line + 1) * N
                    ]

    def send_filtered(j, x, count, sem):
        size = count * 8
        exchange(
            lambda to: out_b.at[j, pl.ds(to * BLOCK + x * 8, size)],
            lambda me: in_b.at[j, pl.ds(me * BLOCK + x * 8, size)],
            b_send.at[sem], b_recv.at[sem], True,
        )

    for j in range(2):
        await_rows(in_a.at[j], BLOCK, a_recv.at[j])
        filtered(j)
        if j == 0:
            send_filtered(j, 0, LINES, 0)
        else:
            for x in range(LINES):
                send_filtered(j, x, 1, 1 + x)
        keep(j, in_b, out_b[j, pl.ds(pl.multiple_of(grid * BLOCK, BLOCK), BLOCK), :])

    def finish(j, x):
        gathered = gather(
            in_b.at[j],
            [unit(x, part, line) for line in range(LINES) for part in range(2)],
        )
        plane = product(weights(4), split(gathered))
        plane = jnp.concatenate([plane[:N], plane[N:]], axis=1)
        potential = product(split(plane), weights(5))
        parts = [potential[:, c * N : (c + 1) * N] for c in range(2)]
        for c in range(2):
            term = parts[c] * received[j, x]
            total[c, x] = term if j == 0 else total[c, x] + term

        if j == 1:

            @pl.when(upper == 1)
            def _():
                for c in range(2):
                    pass_on(
                        total.at[c, x], returned_hbm.at[c, x], ret_send.at[0], ret_recv.at[0], partner
                    )

        back[j, x] = parts[0] * own[0, x] + parts[1] * own[1, x]

        @pl.when(lower)
        def _():
            pass_on(back.at[j, x], returned_hbm.at[j, x], ret_send.at[0], ret_recv.at[0], around(-1))
            if j == 1:
                for c in range(2):
                    stay(total.at[c, x], kept_hbm.at[c, x], kept_recv.at[0])

        @pl.when(upper_even)
        def _():
            stay(back.at[j, x], kept_hbm.at[j, x], kept_recv.at[0])

        @pl.when(upper_odd)
        def _():
            pass_on(back.at[j, x], kept_hbm.at[j, x], kept_send.at[0], kept_recv.at[0], around(-2))

    await_rows(in_b.at[0], BLOCK, b_recv.at[0])
    for x in range(LINES):
        finish(0, x)
    for x in range(LINES):
        await_rows(in_b.at[1], 8, b_recv.at[1 + x])
        finish(1, x)

    await_copy(own, shift_send.at[0])
    for j in range(2):
        await_rows(in_a.at[j], BLOCK, a_send.at[j])
    await_rows(in_b.at[0], BLOCK, b_send.at[0])
    for x in range(LINES):
        await_rows(in_b.at[1], 8, b_send.at[1 + x])

    @pl.when(upper_odd)
    def _():
        await_copy(own, lent_send.at[0])
        await_copy(back, kept_send.at[0])

    await_copy(back, ret_send.at[0])
    await_copy(kept_hbm, kept_recv.at[0])
    await_copy(returned_hbm, ret_recv.at[0])


def per_device(orbitals, table):
    slab = (2, LINES, N, N)
    block = (2, PEERS, BLOCK, N)
    flat = (2, PEERS * BLOCK, N)
    f32 = jnp.float32
    dma = pltpu.SemaphoreType.DMA
    kept, returned = pl.pallas_call(
        kernel,
        out_shape=[jax.ShapeDtypeStruct(slab, f32)] * 2,
        in_specs=[pl.BlockSpec(memory_space=pltpu.HBM)] * 2,
        out_specs=[pl.BlockSpec(memory_space=pltpu.HBM)] * 2,
        scratch_shapes=[
            pltpu.VMEM(slab, f32),
            pltpu.VMEM(slab, f32),
            pltpu.VMEM(table.shape, f32),
            pltpu.VMEM((table.shape[0], 2, 2 * N, 2 * N), jnp.bfloat16),
            pltpu.VMEM(slab, f32),
            pltpu.VMEM((N, LINES * N), f32),
            pltpu.VMEM(block, f32),
            pltpu.VMEM(flat, f32),
            pltpu.VMEM(flat, f32),
            pltpu.VMEM(flat, f32),
            pltpu.VMEM(slab, f32),
            pltpu.VMEM(slab, f32),
            dma((2,)),
            dma((2, LINES)),
            dma((2, LINES)),
            dma((1,)),
            dma((1,)),
            dma((2,)),
            dma((2,)),
            dma((1 + LINES,)),
            dma((1 + LINES,)),
            dma((1,)),
            dma((1,)),
            dma((1,)),
            dma((1,)),
        ],
        compiler_params=pltpu.CompilerParams(
            collective_id=0, has_side_effects=True, vmem_limit_bytes=int(52.65 * 2**20)
        ),
    )(orbitals, table)
    return kept + returned


def solution(mesh):
    body = jax.shard_map(
        per_device,
        mesh=mesh,
        in_specs=(P("band", "grid", None, None), P()),
        out_specs=P("band", "grid", None, None),
        check_vma=False,
    )
    constants = tables()
    return lambda orbitals: body(orbitals, jnp.asarray(constants))
```

```python
import functools
import math

import jax
import jax.numpy as jnp
import numpy as np
from jax import lax
from jax.experimental import pallas as pl
from jax.experimental.pallas import tpu as pltpu
from jax.sharding import PartitionSpec as P

screening = 0.0428
MESH = pl.DeviceIdType.MESH
N = 128
LINES = 4
PEERS = 32
BANDS = 8
BLOCK = 8 * LINES


def complex_matrix(sign):
    points = np.arange(N)
    angle = (points[:, None] * points[None, :] % N) * (2.0 * math.pi / N)
    cosine, sine = np.cos(angle), sign * np.sin(angle)
    return np.block([[cosine, -sine], [sine, cosine]])


def peer_major():
    peer, part, line = np.meshgrid(np.arange(PEERS), np.arange(2), np.arange(LINES), indexing="ij")
    return (part * N + peer * LINES + line).reshape(-1)


def line_major():
    line, part, peer = np.meshgrid(np.arange(LINES), np.arange(2), np.arange(PEERS), indexing="ij")
    return (part * N + peer * LINES + line).reshape(-1)


def tables():
    forward, inverse = complex_matrix(-1), complex_matrix(1)
    peers, lines = peer_major(), line_major()
    return np.stack(
        [
            forward.T,
            forward[peers],
            forward[:, lines],
            inverse[lines],
            inverse[:, lines],
            inverse.T,
        ]
    ).astype(np.float32)


def split(x):
    high = x.astype(jnp.bfloat16)
    return high, (x - high.astype(jnp.float32)).astype(jnp.bfloat16)


def product(a, b):
    dot = functools.partial(jnp.dot, preferred_element_type=jnp.float32)
    left = jnp.concatenate([a[0], a[0], a[1]], axis=1)
    return dot(left, jnp.concatenate([b[0], b[1], b[0]], axis=0))


def signed(index):
    return jnp.where(index < N // 2, index, index - N).astype(jnp.float32) * (2.0 * math.pi / N)


def filter_values(me):
    shape = (N, LINES * N)
    lane = lax.broadcasted_iota(jnp.int32, shape, 1)
    kx = signed(lax.broadcasted_iota(jnp.int32, shape, 0))
    ky = signed(me * LINES + lane // N)
    kz = signed(lane % N)
    square = kx * kx + ky * ky + kz * kz
    positive = square > 0
    safe = jnp.where(positive, square, 1.0)
    value = 4.0 * math.pi * (1.0 - jnp.exp(-safe / (4.0 * screening * screening))) / safe
    value = jnp.where(positive, value, math.pi / (screening * screening))
    return value * (-0.25 / float(N * N * N))


def kernel(
    orb_hbm, table_hbm, kept_hbm, returned_hbm,
    home, own, exact, table, received, filt, out_a, in_a, out_b, in_b, back, total,
    table_sem, own_recv, received_recv, shift_send, lent_send,
    a_send, a_recv, b_send, b_recv, ret_send, ret_recv, kept_send, kept_recv,
):
    grid, band = lax.axis_index("grid"), lax.axis_index("band")
    upper, odd = lax.div(grid, PEERS // 2), lax.rem(band, 2)
    partner = band + 1 - 2 * odd
    lower = upper == 0
    lower_band = band + upper * (partner - band)
    upper_band = band + (1 - upper) * (partner - band)
    upper_even = upper * (1 - odd) == 1
    upper_odd = upper * odd == 1

    def around(by):
        return lax.rem(band + (by + BANDS) % BANDS, BANDS)

    def peer(k):
        to = grid + k
        to = jnp.where(to >= PEERS, to - PEERS, to)
        return to, {"band": jnp.where(to >= PEERS // 2, upper_band, lower_band), "grid": to}

    load_home = pltpu.make_async_copy(orb_hbm, home, table_sem.at[1])
    load_home.start()
    load_table = pltpu.make_async_copy(table_hbm, exact, table_sem.at[0])
    load_table.start()

    barrier = pltpu.get_barrier_semaphore()

    def greet_band(to):
        pl.semaphore_signal(barrier, inc=1, device_id={"band": to}, device_id_type=MESH)

    @pl.when(lower)
    def _():
        greet_band(around(1))
        greet_band(around(-1))

    @pl.when(upper == 1)
    def _():
        greet_band(partner)

    @pl.when(upper_odd)
    def _():
        greet_band(around(2))
        greet_band(around(-2))

    def greet(k, carry):
        pl.semaphore_signal(barrier, inc=1, device_id=peer(k)[1], device_id_type=MESH)
        return carry

    lax.fori_loop(1, PEERS, greet, 0)
    pl.semaphore_wait(barrier, PEERS - 1 + (1 - upper) * 2 + upper * (1 + 2 * odd))

    load_home.wait()

    def pass_on(source, target, send_sem, recv_sem, to):
        pltpu.make_async_remote_copy(
            src_ref=source, dst_ref=target, send_sem=send_sem, recv_sem=recv_sem,
            device_id={"band": to}, device_id_type=MESH,
        ).start()

    def stay(source, target, sem):
        pltpu.make_async_copy(source, target, sem).start()

    def await_copy(ref, sem):
        pltpu.make_async_copy(ref, ref, sem).wait()

    pairs = [(c, x) for x in range(LINES) for c in range(2)]
    slabs = [(j, x) for j in range(2) for x in range(LINES)]

    @pl.when(lower)
    def _():
        for j, x in slabs:
            pass_on(
                home.at[j, x], received.at[j, x], shift_send.at[0], received_recv.at[j, x], around(1)
            )
        for c, x in pairs:
            stay(home.at[c, x], own.at[c, x], own_recv.at[c, x])

    @pl.when(upper == 1)
    def _():
        for c, x in pairs:
            pass_on(home.at[c, x], own.at[c, x], shift_send.at[0], own_recv.at[c, x], partner)

    @pl.when(upper_even)
    def _():
        for j, x in slabs:
            stay(home.at[j, x], received.at[j, x], received_recv.at[j, x])

    @pl.when(upper_odd)
    def _():
        for j, x in slabs:
            pass_on(
                home.at[j, x], received.at[j, x], lent_send.at[0], received_recv.at[j, x], around(2)
            )

    def split_table(index):
        table[index, 0], table[index, 1] = split(exact[index])

    def prepare_return():
        filt[...] = filter_values(grid)
        for index in range(2, 6):
            split_table(index)

    load_table.wait()
    split_table(0)
    split_table(1)

    def exchange(source, target, send_sem, recv_sem, by_core=False):
        def send(to, device):
            pltpu.make_async_remote_copy(
                src_ref=source(to), dst_ref=target(grid),
                send_sem=send_sem, recv_sem=recv_sem,
                device_id=device, device_id_type=MESH,
            ).start()

        def next_peer(k, carry):
            send(*peer(k))
            return carry

        def next_chip(i, core):
            chip = lax.div(grid, 2) + i
            chip = jnp.where(chip >= PEERS // 2, chip - PEERS // 2, chip)
            to = chip * 2 + core

            @pl.when(to != grid)
            def _():
                group = jnp.where(chip >= PEERS // 4, upper_band, lower_band)
                send(to, {"band": group, "grid": to})

            return core

        if by_core:
            for core in range(2):
                lax.fori_loop(0, PEERS // 2, next_chip, core)
        else:
            lax.fori_loop(1, PEERS, next_peer, 0)

    def await_rows(target, rows, sem):
        some = target.at[pl.ds(0, (PEERS - 1) * rows)]
        pltpu.make_async_copy(some, some, sem).wait()

    def gather(target, units):
        return jnp.concatenate(
            [target[pl.ds(unit, PEERS, stride=BLOCK), :] for unit in units], axis=0
        )

    def weights(index):
        return table[index, 0], table[index, 1]

    def unit(x, part, line):
        return x * 8 + part * LINES + line

    def spectra(j, planes):
        partner = received[j, planes]
        count = partner.shape[0]
        field = jnp.concatenate(
            [(own[c, planes] * partner).reshape(count * N, N) for c in range(2)], axis=1
        )
        lines = product(split(field), weights(0))
        stacked = jnp.concatenate(
            [
                jnp.concatenate(
                    [lines[x * N : (x + 1) * N, c * N : (c + 1) * N] for x in range(count)], axis=1
                )
                for c in range(2)
            ],
            axis=0,
        )
        result = product(weights(1), split(stacked)).reshape(PEERS, 8, count * N)
        for i in range(count):
            x = planes.start + i
            out_a[j, :, x * 8 : (x + 1) * 8, :] = result[:, :, i * N : (i + 1) * N]

    def send_spectra(j, planes):
        rows = pl.ds(planes.start * 8, (planes.stop - planes.start) * 8)
        first = planes.start * 8
        size = (planes.stop - planes.start) * 8
        exchange(
            lambda to: out_a.at[j, to, rows],
            lambda me: in_a.at[j, pl.ds(me * BLOCK + first, size)],
            a_send.at[j], a_recv.at[j],
        )

    def keep(j, target, block):
        target[j, pl.ds(pl.multiple_of(grid * BLOCK, BLOCK), BLOCK), :] = block

    for x in range(LINES):
        for c in range(2):
            await_copy(own.at[c, x], own_recv.at[c, x])
        await_copy(received.at[0, x], received_recv.at[0, x])
        spectra(0, slice(x, x + 1))
        send_spectra(0, slice(x, x + 1))
    keep(0, in_a, out_a[0, grid])
    for x in range(LINES):
        await_copy(received.at[1, x], received_recv.at[1, x])
    spectra(1, slice(0, LINES))
    send_spectra(1, slice(0, LINES))
    keep(1, in_a, out_a[1, grid])
    prepare_return()

    def filtered(j):
        gathered = jnp.concatenate(
            [
                gather(
                    in_a.at[j],
                    [unit(x, part, line) for x in range(LINES) for part in range(2)],
                )
                for line in range(LINES)
            ],
            axis=1,
        )
        spectrum = product(weights(2), split(gathered))
        values = filt[...]
        spectrum = jnp.concatenate([spectrum[:N] * values, spectrum[N:] * values], axis=0)
        result = product(weights(3), split(spectrum))
        target = out_b.at[j]
        for x in range(LINES):
            for part in range(2):
                first = (x * 2 + part) * PEERS
                for line in range(LINES):
                    target[pl.ds(unit(x, part, line), PEERS, stride=BLOCK), :] = result[
                        first : first + PEERS, line * N : (line + 1) * N
                    ]

    def send_filtered(j, x, count, sem):
        size = count * 8
        exchange(
            lambda to: out_b.at[j, pl.ds(to * BLOCK + x * 8, size)],
            lambda me: in_b.at[j, pl.ds(me * BLOCK + x * 8, size)],
            b_send.at[sem], b_recv.at[sem], True,
        )

    for j in range(2):
        await_rows(in_a.at[j], BLOCK, a_recv.at[j])
        filtered(j)
        if j == 0:
            send_filtered(j, 0, LINES, 0)
        else:
            for x in range(LINES):
                send_filtered(j, x, 1, 1 + x)
        keep(j, in_b, out_b[j, pl.ds(pl.multiple_of(grid * BLOCK, BLOCK), BLOCK), :])

    def finish(j, x):
        gathered = gather(
            in_b.at[j],
            [unit(x, part, line) for line in range(LINES) for part in range(2)],
        )
        plane = product(weights(4), split(gathered))
        plane = jnp.concatenate([plane[:N], plane[N:]], axis=1)
        potential = product(split(plane), weights(5))
        parts = [potential[:, c * N : (c + 1) * N] for c in range(2)]
        for c in range(2):
            term = parts[c] * received[j, x]
            total[c, x] = term if j == 0 else total[c, x] + term

        if j == 1:

            @pl.when(upper == 1)
            def _():
                for c in range(2):
                    pass_on(
                        total.at[c, x], returned_hbm.at[c, x], ret_send.at[0], ret_recv.at[0], partner
                    )

        back[j, x] = parts[0] * own[0, x] + parts[1] * own[1, x]

        @pl.when(lower)
        def _():
            pass_on(back.at[j, x], returned_hbm.at[j, x], ret_send.at[0], ret_recv.at[0], around(-1))
            if j == 1:
                for c in range(2):
                    stay(total.at[c, x], kept_hbm.at[c, x], kept_recv.at[0])

        @pl.when(upper_even)
        def _():
            stay(back.at[j, x], kept_hbm.at[j, x], kept_recv.at[0])

        @pl.when(upper_odd)
        def _():
            pass_on(back.at[j, x], kept_hbm.at[j, x], kept_send.at[0], kept_recv.at[0], around(-2))

    await_rows(in_b.at[0], BLOCK, b_recv.at[0])
    for x in range(LINES):
        finish(0, x)
    for x in range(LINES):
        await_rows(in_b.at[1], 8, b_recv.at[1 + x])
        finish(1, x)

    await_copy(own, shift_send.at[0])
    for j in range(2):
        await_rows(in_a.at[j], BLOCK, a_send.at[j])
    await_rows(in_b.at[0], BLOCK, b_send.at[0])
    for x in range(LINES):
        await_rows(in_b.at[1], 8, b_send.at[1 + x])

    @pl.when(upper_odd)
    def _():
        await_copy(own, lent_send.at[0])
        await_copy(back, kept_send.at[0])

    await_copy(back, ret_send.at[0])
    await_copy(kept_hbm, kept_recv.at[0])
    await_copy(returned_hbm, ret_recv.at[0])


def per_device(orbitals, table):
    slab = (2, LINES, N, N)
    block = (2, PEERS, BLOCK, N)
    flat = (2, PEERS * BLOCK, N)
    f32 = jnp.float32
    dma = pltpu.SemaphoreType.DMA
    kept, returned = pl.pallas_call(
        kernel,
        out_shape=[jax.ShapeDtypeStruct(slab, f32)] * 2,
        in_specs=[pl.BlockSpec(memory_space=pltpu.HBM)] * 2,
        out_specs=[pl.BlockSpec(memory_space=pltpu.HBM)] * 2,
        scratch_shapes=[
            pltpu.VMEM(slab, f32),
            pltpu.VMEM(slab, f32),
            pltpu.VMEM(table.shape, f32),
            pltpu.VMEM((table.shape[0], 2, 2 * N, 2 * N), jnp.bfloat16),
            pltpu.VMEM(slab, f32),
            pltpu.VMEM((N, LINES * N), f32),
            pltpu.VMEM(block, f32),
            pltpu.VMEM(flat, f32),
            pltpu.VMEM(flat, f32),
            pltpu.VMEM(flat, f32),
            pltpu.VMEM(slab, f32),
            pltpu.VMEM(slab, f32),
            dma((2,)),
            dma((2, LINES)),
            dma((2, LINES)),
            dma((1,)),
            dma((1,)),
            dma((2,)),
            dma((2,)),
            dma((1 + LINES,)),
            dma((1 + LINES,)),
            dma((1,)),
            dma((1,)),
            dma((1,)),
            dma((1,)),
        ],
        compiler_params=pltpu.CompilerParams(
            collective_id=0, has_side_effects=True, vmem_limit_bytes=int(52.65 * 2**20)
        ),
    )(orbitals, table)
    return kept + returned


def solution(mesh):
    body = jax.shard_map(
        per_device,
        mesh=mesh,
        in_specs=(P("band", "grid", None, None), P()),
        out_specs=P("band", "grid", None, None),
        check_vma=False,
    )
    constants = tables()
    return lambda orbitals: body(orbitals, jnp.asarray(constants))
```

```python
import functools
import math

import jax
import jax.numpy as jnp
import numpy as np
from jax import lax
from jax.experimental import pallas as pl
from jax.experimental.pallas import tpu as pltpu
from jax.sharding import PartitionSpec as P

screening = 0.0428
MESH = pl.DeviceIdType.MESH
N = 128
LINES = 4
PEERS = 32
BANDS = 8
BLOCK = 8 * LINES


def complex_matrix(sign):
    points = np.arange(N)
    angle = (points[:, None] * points[None, :] % N) * (2.0 * math.pi / N)
    cosine, sine = np.cos(angle), sign * np.sin(angle)
    return np.block([[cosine, -sine], [sine, cosine]])


def peer_major():
    peer, part, line = np.meshgrid(np.arange(PEERS), np.arange(2), np.arange(LINES), indexing="ij")
    return (part * N + peer * LINES + line).reshape(-1)


def line_major():
    line, part, peer = np.meshgrid(np.arange(LINES), np.arange(2), np.arange(PEERS), indexing="ij")
    return (part * N + peer * LINES + line).reshape(-1)


def tables():
    forward, inverse = complex_matrix(-1), complex_matrix(1)
    peers, lines = peer_major(), line_major()
    return np.stack(
        [
            forward.T,
            forward[peers],
            forward[:, lines],
            inverse[lines],
            inverse[:, lines],
            inverse.T,
        ]
    ).astype(np.float32)


def split(x):
    high = x.astype(jnp.bfloat16)
    return high, (x - high.astype(jnp.float32)).astype(jnp.bfloat16)


def product(a, b):
    dot = functools.partial(jnp.dot, preferred_element_type=jnp.float32)
    return dot(a[0], b[0]) + (dot(a[0], b[1]) + dot(a[1], b[0]))


def signed(index):
    return jnp.where(index < N // 2, index, index - N).astype(jnp.float32) * (2.0 * math.pi / N)


def filter_values(me):
    shape = (N, LINES * N)
    lane = lax.broadcasted_iota(jnp.int32, shape, 1)
    kx = signed(lax.broadcasted_iota(jnp.int32, shape, 0))
    ky = signed(me * LINES + lane // N)
    kz = signed(lane % N)
    square = kx * kx + ky * ky + kz * kz
    positive = square > 0
    safe = jnp.where(positive, square, 1.0)
    value = 4.0 * math.pi * (1.0 - jnp.exp(-safe / (4.0 * screening * screening))) / safe
    value = jnp.where(positive, value, math.pi / (screening * screening))
    return value * (-0.25 / float(N * N * N))


def kernel(
    orb_hbm, table_hbm, kept_hbm, returned_hbm,
    home, own, exact, table, received, filt, out_a, in_a, out_b, in_b, back, total,
    table_sem, own_recv, received_recv, shift_send, lent_send,
    a_send, a_recv, b_send, b_recv, ret_send, ret_recv, kept_send, kept_recv,
):
    grid, band = lax.axis_index("grid"), lax.axis_index("band")
    upper, odd = lax.div(grid, PEERS // 2), lax.rem(band, 2)
    partner = band + 1 - 2 * odd
    lower = upper == 0
    lower_band = band + upper * (partner - band)
    upper_band = band + (1 - upper) * (partner - band)
    upper_even = upper * (1 - odd) == 1
    upper_odd = upper * odd == 1

    def around(by):
        return lax.rem(band + (by + BANDS) % BANDS, BANDS)

    def peer(k):
        to = grid + k
        to = jnp.where(to >= PEERS, to - PEERS, to)
        return to, {"band": jnp.where(to >= PEERS // 2, upper_band, lower_band), "grid": to}

    load_home = pltpu.make_async_copy(orb_hbm, home, table_sem.at[1])
    load_home.start()
    load_table = pltpu.make_async_copy(table_hbm, exact, table_sem.at[0])
    load_table.start()

    barrier = pltpu.get_barrier_semaphore()

    def greet_band(to):
        pl.semaphore_signal(barrier, inc=1, device_id={"band": to}, device_id_type=MESH)

    @pl.when(lower)
    def _():
        greet_band(around(1))
        greet_band(around(-1))

    @pl.when(upper == 1)
    def _():
        greet_band(partner)

    @pl.when(upper_odd)
    def _():
        greet_band(around(2))
        greet_band(around(-2))

    def greet(k, carry):
        pl.semaphore_signal(barrier, inc=1, device_id=peer(k)[1], device_id_type=MESH)
        return carry

    lax.fori_loop(1, PEERS, greet, 0)
    pl.semaphore_wait(barrier, PEERS - 1 + (1 - upper) * 2 + upper * (1 + 2 * odd))

    load_home.wait()

    def pass_on(source, target, send_sem, recv_sem, to):
        pltpu.make_async_remote_copy(
            src_ref=source, dst_ref=target, send_sem=send_sem, recv_sem=recv_sem,
            device_id={"band": to}, device_id_type=MESH,
        ).start()

    def stay(source, target, sem):
        pltpu.make_async_copy(source, target, sem).start()

    def await_copy(ref, sem):
        pltpu.make_async_copy(ref, ref, sem).wait()

    pairs = [(c, x) for x in range(LINES) for c in range(2)]
    slabs = [(j, x) for j in range(2) for x in range(LINES)]

    @pl.when(lower)
    def _():
        for j, x in slabs:
            pass_on(
                home.at[j, x], received.at[j, x], shift_send.at[0], received_recv.at[j, x], around(1)
            )
        for c, x in pairs:
            stay(home.at[c, x], own.at[c, x], own_recv.at[c, x])

    @pl.when(upper == 1)
    def _():
        for c, x in pairs:
            pass_on(home.at[c, x], own.at[c, x], shift_send.at[0], own_recv.at[c, x], partner)

    @pl.when(upper_even)
    def _():
        for j, x in slabs:
            stay(home.at[j, x], received.at[j, x], received_recv.at[j, x])

    @pl.when(upper_odd)
    def _():
        for j, x in slabs:
            pass_on(
                home.at[j, x], received.at[j, x], lent_send.at[0], received_recv.at[j, x], around(2)
            )

    def split_table(index):
        table[index, 0], table[index, 1] = split(exact[index])

    def prepare_return():
        filt[...] = filter_values(grid)
        for index in range(2, 6):
            split_table(index)

    load_table.wait()
    split_table(0)
    split_table(1)

    def exchange(source, target, send_sem, recv_sem, by_core=False):
        def send(to, device):
            pltpu.make_async_remote_copy(
                src_ref=source(to), dst_ref=target(grid),
                send_sem=send_sem, recv_sem=recv_sem,
                device_id=device, device_id_type=MESH,
            ).start()

        def next_peer(k, carry):
            send(*peer(k))
            return carry

        def next_chip(i, core):
            chip = lax.div(grid, 2) + i
            chip = jnp.where(chip >= PEERS // 2, chip - PEERS // 2, chip)
            to = chip * 2 + core

            @pl.when(to != grid)
            def _():
                group = jnp.where(chip >= PEERS // 4, upper_band, lower_band)
                send(to, {"band": group, "grid": to})

            return core

        if by_core:
            for core in range(2):
                lax.fori_loop(0, PEERS // 2, next_chip, core)
        else:
            lax.fori_loop(1, PEERS, next_peer, 0)

    def await_rows(target, rows, sem):
        some = target.at[pl.ds(0, (PEERS - 1) * rows)]
        pltpu.make_async_copy(some, some, sem).wait()

    def gather(target, units):
        return jnp.concatenate(
            [target[pl.ds(unit, PEERS, stride=BLOCK), :] for unit in units], axis=0
        )

    def weights(index):
        return table[index, 0], table[index, 1]

    def unit(x, part, line):
        return x * 8 + part * LINES + line

    def spectra(j, planes):
        partner = received[j, planes]
        count = partner.shape[0]
        field = jnp.concatenate(
            [(own[c, planes] * partner).reshape(count * N, N) for c in range(2)], axis=1
        )
        lines = product(split(field), weights(0))
        stacked = jnp.concatenate(
            [
                jnp.concatenate(
                    [lines[x * N : (x + 1) * N, c * N : (c + 1) * N] for x in range(count)], axis=1
                )
                for c in range(2)
            ],
            axis=0,
        )
        result = product(weights(1), split(stacked)).reshape(PEERS, 8, count * N)
        for i in range(count):
            x = planes.start + i
            out_a[j, :, x * 8 : (x + 1) * 8, :] = result[:, :, i * N : (i + 1) * N]

    def send_spectra(j, planes):
        rows = pl.ds(planes.start * 8, (planes.stop - planes.start) * 8)
        first = planes.start * 8
        size = (planes.stop - planes.start) * 8
        exchange(
            lambda to: out_a.at[j, to, rows],
            lambda me: in_a.at[j, pl.ds(me * BLOCK + first, size)],
            a_send.at[j], a_recv.at[j],
        )

    def keep(j, target, block):
        target[j, pl.ds(pl.multiple_of(grid * BLOCK, BLOCK), BLOCK), :] = block

    for x in range(LINES):
        for c in range(2):
            await_copy(own.at[c, x], own_recv.at[c, x])
        await_copy(received.at[0, x], received_recv.at[0, x])
        spectra(0, slice(x, x + 1))
        send_spectra(0, slice(x, x + 1))
    keep(0, in_a, out_a[0, grid])
    for x in range(LINES):
        await_copy(received.at[1, x], received_recv.at[1, x])
    spectra(1, slice(0, LINES))
    send_spectra(1, slice(0, LINES))
    keep(1, in_a, out_a[1, grid])
    prepare_return()

    def filtered(j):
        gathered = jnp.concatenate(
            [
                gather(
                    in_a.at[j],
                    [unit(x, part, line) for x in range(LINES) for part in range(2)],
                )
                for line in range(LINES)
            ],
            axis=1,
        )
        spectrum = product(weights(2), split(gathered))
        values = filt[...]
        spectrum = jnp.concatenate([spectrum[:N] * values, spectrum[N:] * values], axis=0)
        result = product(weights(3), split(spectrum))
        target = out_b.at[j]
        for x in range(LINES):
            for part in range(2):
                first = (x * 2 + part) * PEERS
                for line in range(LINES):
                    target[pl.ds(unit(x, part, line), PEERS, stride=BLOCK), :] = result[
                        first : first + PEERS, line * N : (line + 1) * N
                    ]

    def send_filtered(j, x, count, sem):
        size = count * 8
        exchange(
            lambda to: out_b.at[j, pl.ds(to * BLOCK + x * 8, size)],
            lambda me: in_b.at[j, pl.ds(me * BLOCK + x * 8, size)],
            b_send.at[sem], b_recv.at[sem], sem > 0,
        )

    for j in range(2):
        await_rows(in_a.at[j], BLOCK, a_recv.at[j])
        filtered(j)
        if j == 0:
            send_filtered(j, 0, LINES, 0)
        else:
            for x in range(LINES):
                send_filtered(j, x, 1, 1 + x)
        keep(j, in_b, out_b[j, pl.ds(pl.multiple_of(grid * BLOCK, BLOCK), BLOCK), :])

    def finish(j, x):
        gathered = gather(
            in_b.at[j],
            [unit(x, part, line) for line in range(LINES) for part in range(2)],
        )
        plane = product(weights(4), split(gathered))
        plane = jnp.concatenate([plane[:N], plane[N:]], axis=1)
        potential = product(split(plane), weights(5))
        parts = [potential[:, c * N : (c + 1) * N] for c in range(2)]
        for c in range(2):
            term = parts[c] * received[j, x]
            total[c, x] = term if j == 0 else total[c, x] + term

        if j == 1:

            @pl.when(upper == 1)
            def _():
                for c in range(2):
                    pass_on(
                        total.at[c, x], returned_hbm.at[c, x], ret_send.at[0], ret_recv.at[0], partner
                    )

        back[j, x] = parts[0] * own[0, x] + parts[1] * own[1, x]

        @pl.when(lower)
        def _():
            pass_on(back.at[j, x], returned_hbm.at[j, x], ret_send.at[0], ret_recv.at[0], around(-1))
            if j == 1:
                for c in range(2):
                    stay(total.at[c, x], kept_hbm.at[c, x], kept_recv.at[0])

        @pl.when(upper_even)
        def _():
            stay(back.at[j, x], kept_hbm.at[j, x], kept_recv.at[0])

        @pl.when(upper_odd)
        def _():
            pass_on(back.at[j, x], kept_hbm.at[j, x], kept_send.at[0], kept_recv.at[0], around(-2))

    await_rows(in_b.at[0], BLOCK, b_recv.at[0])
    for x in range(LINES):
        finish(0, x)
    for x in range(LINES):
        await_rows(in_b.at[1], 8, b_recv.at[1 + x])
        finish(1, x)

    await_copy(own, shift_send.at[0])
    for j in range(2):
        await_rows(in_a.at[j], BLOCK, a_send.at[j])
    await_rows(in_b.at[0], BLOCK, b_send.at[0])
    for x in range(LINES):
        await_rows(in_b.at[1], 8, b_send.at[1 + x])

    @pl.when(upper_odd)
    def _():
        await_copy(own, lent_send.at[0])
        await_copy(back, kept_send.at[0])

    await_copy(back, ret_send.at[0])
    await_copy(kept_hbm, kept_recv.at[0])
    await_copy(returned_hbm, ret_recv.at[0])


def per_device(orbitals, table):
    slab = (2, LINES, N, N)
    block = (2, PEERS, BLOCK, N)
    flat = (2, PEERS * BLOCK, N)
    f32 = jnp.float32
    dma = pltpu.SemaphoreType.DMA
    kept, returned = pl.pallas_call(
        kernel,
        out_shape=[jax.ShapeDtypeStruct(slab, f32)] * 2,
        in_specs=[pl.BlockSpec(memory_space=pltpu.HBM)] * 2,
        out_specs=[pl.BlockSpec(memory_space=pltpu.HBM)] * 2,
        scratch_shapes=[
            pltpu.VMEM(slab, f32),
            pltpu.VMEM(slab, f32),
            pltpu.VMEM(table.shape, f32),
            pltpu.VMEM((table.shape[0], 2, 2 * N, 2 * N), jnp.bfloat16),
            pltpu.VMEM(slab, f32),
            pltpu.VMEM((N, LINES * N), f32),
            pltpu.VMEM(block, f32),
            pltpu.VMEM(flat, f32),
            pltpu.VMEM(flat, f32),
            pltpu.VMEM(flat, f32),
            pltpu.VMEM(slab, f32),
            pltpu.VMEM(slab, f32),
            dma((2,)),
            dma((2, LINES)),
            dma((2, LINES)),
            dma((1,)),
            dma((1,)),
            dma((2,)),
            dma((2,)),
            dma((1 + LINES,)),
            dma((1 + LINES,)),
            dma((1,)),
            dma((1,)),
            dma((1,)),
            dma((1,)),
        ],
        compiler_params=pltpu.CompilerParams(
            collective_id=0, has_side_effects=True, vmem_limit_bytes=int(52.65 * 2**20)
        ),
    )(orbitals, table)
    return kept + returned


def solution(mesh):
    body = jax.shard_map(
        per_device,
        mesh=mesh,
        in_specs=(P("band", "grid", None, None), P()),
        out_specs=P("band", "grid", None, None),
        check_vma=False,
    )
    constants = tables()
    return lambda orbitals: body(orbitals, jnp.asarray(constants))
```
